512 devices in a mesh: section: 2 (over x_hi), gy: 16 (over y, x_lo, core), gx: 16 (over z).
Axes of the slice: x: 4 (x_hi: 2, x_lo: 2; x = x_hi * 2 + x_lo), y: 4, z: 16, core: 2. Of those that a mesh axis runs over, the one named last changes fastest.
Arguments:
- images: bfloat16 [2, 512, 1024, 128], P('section', 'gy', 'gx'), may hold values from -6 to 6
- first_kernel: bfloat16 [3, 3, 128, 128], replicated, may hold values from -0.1875 to 0.1875
- projection: bfloat16 [128, 256], replicated, may hold values from -0.5 to 0.5
- second_kernel: bfloat16 [3, 3, 256, 256], replicated, may hold values from -0.125 to 0.125
- cotangent: bfloat16 [2, 256, 512, 256], P('section', 'gy', 'gx'), may hold values from -0.15625 to 0.15625
Outputs:
- features: bfloat16 [2, 256, 512, 256], P('section', 'gy', 'gx')
- grad_first: float32 [3, 3, 128, 128], replicated
- grad_projection: float32 [128, 256], replicated
- grad_second: float32 [3, 3, 256, 256], replicated
The draws below stay inside these ranges and needn't reach their ends.
All inputs are finite; a program needn't handle non-finite values.
Results may differ from the reference program's by a relative error of at most 0.014.
Values may be sent and summed in bfloat16 or wider, within the bound.
A program may use at most 64 MiB of HBM per device.

```python
import jax
import jax.numpy as jnp

CHANNELS = 128
CHANNELS_WIDE = 256
HEIGHT = 512
WIDTH = 1024
HALF_HEIGHT = 256
HALF_WIDTH = 512


def block_scale(rng, shape, cuts, smallest, high):
    gain = 1.0
    for position, shards_of in cuts:
        draws = jax.random.uniform(jax.random.fold_in(jax.random.fold_in(rng, 6), position), (shards_of,), jnp.float32, smallest / len(cuts), high / len(cuts))
        gain = gain * jnp.repeat(jnp.exp(draws), shape[position] // shards_of).reshape((-1,) + (1,) * (len(shape) - 1 - position))
    return gain


def scatter_about(rng, dims, scale, reach, split=(), kind=jnp.bfloat16):
    level = block_scale(rng, dims, split, -0.22, 0.18) if split else 1.0
    result = jax.random.normal(rng, dims, jnp.float32) * scale * level
    return jnp.minimum(jnp.maximum(result, -reach), reach).astype(kind)


def setup_inputs(seed: int = 0) -> dict:
    seeds = jax.random.split(jax.random.key(seed), 6)
    return {
        "images": scatter_about(seeds[0], (2, HEIGHT, WIDTH, CHANNELS), 1.0, 6.0, ((0, 2), (1, 16), (2, 16))),
        "first_kernel": scatter_about(seeds[1], (3, 3, CHANNELS, CHANNELS), (9 * CHANNELS) ** -0.5, 0.1875),
        "projection": scatter_about(seeds[2], (CHANNELS, CHANNELS_WIDE), CHANNELS ** -0.5, 0.5),
        "second_kernel": scatter_about(seeds[3], (3, 3, CHANNELS_WIDE, CHANNELS_WIDE), (9 * CHANNELS_WIDE) ** -0.5, 0.125),
        "cotangent": scatter_about(seeds[4], (2, HALF_HEIGHT, HALF_WIDTH, CHANNELS_WIDE), (10.0 * (2 * HEIGHT * WIDTH) ** -0.5), 0.15625, ((0, 2), (1, 16), (2, 16))),
    }


def silu_slope(values):
    sigma = jax.nn.sigmoid(values)
    return sigma * (1.0 + values * (1.0 - sigma))


def product(left, right):
    return jnp.dot(left.astype(jnp.float32), right.astype(jnp.float32))


def pad_field(field):
    return jnp.pad(field, ((1, 1), (1, 1), (0, 0)))


def conv_forward(padded, kernel, row_count, col_count):
    total = jnp.zeros((row_count * col_count, kernel.shape[3]), jnp.float32)
    for row_tap in range(3):
        for col_tap in range(3):
            piece = padded[row_tap:row_tap + row_count, col_tap:col_tap + col_count].reshape(row_count * col_count, padded.shape[2])
            total = total + product(piece, kernel[row_tap, col_tap])
    return total


def conv_slopes(padded, slope, row_count, col_count):
    pieces = []
    for row_tap in range(3):
        for col_tap in range(3):
            piece = padded[row_tap:row_tap + row_count, col_tap:col_tap + col_count].reshape(row_count * col_count, padded.shape[2])
            pieces.append(product(piece.T, slope))
    return jnp.stack(pieces).reshape(3, 3, padded.shape[2], slope.shape[1])


def conv_back(padded, kernel, row_count, col_count):
    total = jnp.zeros((row_count * col_count, kernel.shape[2]), jnp.float32)
    for row_tap in range(3):
        for col_tap in range(3):
            piece = padded[2 - row_tap:2 - row_tap + row_count, 2 - col_tap:2 - col_tap + col_count].reshape(row_count * col_count, padded.shape[2])
            total = total + product(piece, kernel[row_tap, col_tap].T)
    return total


def reference(images, first_kernel, projection, second_kernel, cotangent):
    outputs = []
    grad_first = jnp.zeros((3, 3, CHANNELS, CHANNELS), jnp.float32)
    grad_projection = jnp.zeros((CHANNELS, CHANNELS_WIDE), jnp.float32)
    grad_second = jnp.zeros((3, 3, CHANNELS_WIDE, CHANNELS_WIDE), jnp.float32)
    for source in range(2):
        padded_in = pad_field(images[source])
        before_one = conv_forward(padded_in, first_kernel, HEIGHT, WIDTH)
        hidden = jax.nn.silu(before_one).astype(jnp.bfloat16).reshape(HEIGHT, WIDTH, CHANNELS)
        pooled = (hidden.astype(jnp.float32).reshape(HALF_HEIGHT, 2, HALF_WIDTH, 2, CHANNELS).sum(axis=(1, 3)) * 0.25).astype(jnp.bfloat16)
        flat_pool = pooled.reshape(HALF_HEIGHT * HALF_WIDTH, CHANNELS)
        middle = product(flat_pool, projection).astype(jnp.bfloat16)
        padded_mid = pad_field(middle.reshape(HALF_HEIGHT, HALF_WIDTH, CHANNELS_WIDE))
        before_two = conv_forward(padded_mid, second_kernel, HALF_HEIGHT, HALF_WIDTH)
        outputs.append(jax.nn.silu(before_two).astype(jnp.bfloat16).reshape(HALF_HEIGHT, HALF_WIDTH, CHANNELS_WIDE))
        upstream = cotangent[1 - source].astype(jnp.float32).reshape(HALF_HEIGHT * HALF_WIDTH, CHANNELS_WIDE)
        slope_two = (upstream * silu_slope(before_two)).astype(jnp.bfloat16)
        grad_second = grad_second + conv_slopes(padded_mid, slope_two, HALF_HEIGHT, HALF_WIDTH)
        padded_slope = pad_field(slope_two.reshape(HALF_HEIGHT, HALF_WIDTH, CHANNELS_WIDE))
        middle_slope = conv_back(padded_slope, second_kernel, HALF_HEIGHT, HALF_WIDTH).astype(jnp.bfloat16)
        grad_projection = grad_projection + product(flat_pool.T, middle_slope)
        pooled_slope = product(middle_slope, projection.T).astype(jnp.bfloat16).reshape(HALF_HEIGHT, HALF_WIDTH, CHANNELS)
        spread = jnp.broadcast_to((pooled_slope.astype(jnp.float32) * 0.25)[:, None, :, None, :], (HALF_HEIGHT, 2, HALF_WIDTH, 2, CHANNELS)).reshape(HEIGHT * WIDTH, CHANNELS)
        slope_one = (spread * silu_slope(before_one)).astype(jnp.bfloat16)
        grad_first = grad_first + conv_slopes(padded_in, slope_one, HEIGHT, WIDTH)
    features = jnp.stack([outputs[1], outputs[0]])
    return features, grad_first, grad_projection, grad_second
```

```python
import functools

import jax
import jax.numpy as jnp
from jax import lax
from jax.experimental import pallas as pl
from jax.experimental.pallas import tpu as pltpu
from jax.sharding import PartitionSpec as P


MESH = pl.DeviceIdType.MESH
F32, BF16 = jnp.float32, jnp.bfloat16
UNITS = 12
def coords():
    s, g, z = lax.axis_index("section"), lax.axis_index("gy"), lax.axis_index("gx")
    core = lax.rem(g, 2)
    x = s * 2 + lax.rem(lax.div(g, 2), 2)
    y = lax.div(g, 4)
    return x, y, core, z

def dev(x, y, core, z):
    return (lax.div(x, 2), y * 4 + lax.rem(x, 2) * 2 + core, z)

def ar_kernel(chunks, stop, a_ref, out, r0, h0, r1, h1, r2, h2, zb, *sems):
    (s0s, s0r, s1s, s1r, s2s, s2r, zs, zr, gzs, gzr, g2s, g2r, g1s, g1r, g0s, g0r) = sems
    x, y, core, z = coords()
    mod4 = lambda v: lax.rem(v, 4)
    sib = dev(x, y, 1 - core, z)
    barrier = pltpu.get_barrier_semaphore()
    pl.semaphore_signal(barrier, inc=1, device_id=sib, device_id_type=MESH)
    for d in range(1, 4):
        pl.semaphore_signal(barrier, inc=1, device_id=dev(mod4(x + d), y, core, z), device_id_type=MESH)
        pl.semaphore_signal(barrier, inc=1, device_id=dev(x, mod4(y + d), core, z), device_id_type=MESH)
    for d in range(1, 16):
        pl.semaphore_signal(barrier, inc=1, device_id=dev(x, y, core, lax.rem(z + d, 16)), device_id_type=MESH)
    pl.semaphore_wait(barrier, 22)

    mine = pl.ds(pl.multiple_of(core * 128, 128), 128)
    other = pl.ds(pl.multiple_of((1 - core) * 128, 128), 128)
    sends = []

    def push(src, dst, ss, rs, to):
        c = pltpu.make_async_remote_copy(src_ref=src, dst_ref=dst, send_sem=ss, recv_sem=rs, device_id=to, device_id_type=MESH)
        c.start()
        sends.append(c)
        return c

    def axes(yfirst):
        if yfirst:
            return (y, lambda p: dev(x, p, core, z)), (x, lambda p: dev(p, y, core, z))
        return (x, lambda p: dev(p, y, core, z)), (y, lambda p: dev(x, p, core, z))

    def st0(ci, ch):
        u0, n, yf = ch
        us = pl.ds(u0, n)
        return [push(a_ref.at[us, :, other], r0.at[us], s0s.at[ci], s0r.at[ci], sib)]

    def st1(ci, ch, c):
        u0, n, yf = ch
        us = pl.ds(u0, n)
        c[0].wait_recv()
        h0[us] = (a_ref[us, :, mine].astype(F32) + r0[us].astype(F32)).astype(BF16)
        (fm, fd), _ = axes(yf)
        out_c = []
        for d in range(1, 4):
            p = mod4(fm + d)
            out_c.append(push(h0.at[us, pl.ds(pl.multiple_of(p * 64, 64), 64)], r1.at[d - 1, us], s1s.at[ci, d - 1], s1r.at[ci, d - 1], fd(p)))
        return out_c

    def st2(ci, ch, c):
        u0, n, yf = ch
        us = pl.ds(u0, n)
        for k in c:
            k.wait_recv()
        (fm, fd), (sm, sd) = axes(yf)
        h1[us] = (h0[us, pl.ds(pl.multiple_of(fm * 64, 64), 64)].astype(F32) + r1[0, us].astype(F32) + r1[1, us].astype(F32) + r1[2, us].astype(F32)).astype(BF16)
        out_c = []
        for d in range(1, 4):
            p = mod4(sm + d)
            out_c.append(push(h1.at[us, pl.ds(pl.multiple_of(p * 16, 16), 16)], r2.at[d - 1, us], s2s.at[ci, d - 1], s2r.at[ci, d - 1], sd(p)))
        return out_c

    def st3(ci, ch, c):
        u0, n, yf = ch
        us = pl.ds(u0, n)
        for k in c:
            k.wait_recv()
        (fm, fd), (sm, sd) = axes(yf)
        h2[us] = (h1[us, pl.ds(pl.multiple_of(sm * 16, 16), 16)].astype(F32) + r2[0, us].astype(F32) + r2[1, us].astype(F32) + r2[2, us].astype(F32)).astype(BF16)
        for u in range(u0, u0 + n):
            @pl.when(z != u)
            def _():
                pltpu.make_async_remote_copy(src_ref=h2.at[u], dst_ref=zb.at[z], send_sem=zs.at[u], recv_sem=zr, device_id=dev(x, y, core, u), device_id_type=MESH).start()
        return None

    def rows16(yf):
        (fm, fd), (sm, sd) = axes(yf)
        return pl.ds(pl.multiple_of(fm * 64 + sm * 16, 16), 16)

    def rows64(yf):
        (fm, fd), (sm, sd) = axes(yf)
        return pl.ds(pl.multiple_of(fm * 64, 64), 64)

    def st4(ci, ch, c):
        u0, n, yf = ch
        r16 = rows16(yf)
        @pl.when(jnp.logical_and(z >= u0, z < u0 + n))
        def _():
            zb[z] = h2[z]
            pltpu.make_async_copy(zb.at[pl.ds(0, 15)], zb.at[pl.ds(0, 15)], zr).wait()
            tot = zb[0].astype(F32)
            for k in range(1, 16):
                tot = tot + zb[k].astype(F32)
            out[z, r16, mine] = tot.astype(BF16)
            for d in range(1, 16):
                to = lax.rem(z + d, 16)
                pltpu.make_async_remote_copy(src_ref=out.at[z, r16, mine], dst_ref=out.at[z, r16, mine], send_sem=gzs, recv_sem=gzr.at[z], device_id=dev(x, y, core, to), device_id_type=MESH).start()
        return None

    def st5(ci, ch, c):
        u0, n, yf = ch
        us = pl.ds(u0, n)
        r16 = rows16(yf)
        for u in range(u0, u0 + n):
            @pl.when(z != u)
            def _():
                pltpu.make_async_copy(out.at[u, r16, mine], out.at[u, r16, mine], gzr.at[u]).wait()
        (fm, fd), (sm, sd) = axes(yf)
        return [push(out.at[us, r16, mine], out.at[us, r16, mine], g2s.at[ci, d - 1], g2r.at[ci, d - 1], sd(mod4(sm + d))) for d in range(1, 4)]

    def st6(ci, ch, c):
        u0, n, yf = ch
        us = pl.ds(u0, n)
        for k in c:
            k.wait_recv()
        r64 = rows64(yf)
        (fm, fd), (sm, sd) = axes(yf)
        return [push(out.at[us, r64, mine], out.at[us, r64, mine], g1s.at[ci, d - 1], g1r.at[ci, d - 1], fd(mod4(fm + d))) for d in range(1, 4)]

    def st7(ci, ch, c):
        u0, n, yf = ch
        us = pl.ds(u0, n)
        for k in c:
            k.wait_recv()
        return [push(out.at[us, :, mine], out.at[us, :, mine], g0s.at[ci], g0r.at[ci], sib)]

    if stop == 0:
        return
    state = [st0(ci, ch) for ci, ch in enumerate(chunks)]
    for k, st in enumerate((st1, st2, st3, st4, st5, st6, st7)):
        if k + 2 > stop:
            break
        state = [st(ci, ch, state[ci]) for ci, ch in enumerate(chunks)]
    for c in state:
        for e in c or []:
            e.wait_recv()
    for c in sends:
        c.wait_send()
    if stop >= 4:
        for u in range(UNITS):
            @pl.when(z != u)
            def _():
                pltpu.make_async_copy(h2.at[u], h2.at[u], zs.at[u]).wait()
    if stop == 4:
        @pl.when(z < UNITS)
        def _():
            pltpu.make_async_copy(zb.at[pl.ds(0, 15)], zb.at[pl.ds(0, 15)], zr).wait()
    if stop == 5:
        for u in range(UNITS):
            @pl.when(z != u)
            def _():
                pltpu.make_async_copy(h2.at[u], h2.at[u], gzr.at[u]).wait()
    if stop >= 5:
        @pl.when(z < UNITS)
        def _():
            pltpu.make_async_copy(zb.at[pl.ds(0, 15)], zb.at[pl.ds(0, 15)], gzs).wait()

def ar(a, chunks, cid=0, stop=8):
    n = len(chunks)
    D = pltpu.SemaphoreType.DMA
    return pl.pallas_call(
        functools.partial(ar_kernel, chunks, stop),
        out_shape=jax.ShapeDtypeStruct((UNITS, 256, 256), BF16),
        in_specs=[pl.BlockSpec(memory_space=pltpu.VMEM)],
        out_specs=pl.BlockSpec(memory_space=pltpu.VMEM),
        scratch_shapes=[
            pltpu.VMEM((UNITS, 256, 128), BF16), pltpu.VMEM((UNITS, 256, 128), BF16),
            pltpu.VMEM((3, UNITS, 64, 128), BF16), pltpu.VMEM((UNITS, 64, 128), BF16),
            pltpu.VMEM((3, UNITS, 16, 128), BF16), pltpu.VMEM((UNITS, 16, 128), BF16),
            pltpu.VMEM((16, 16, 128), BF16),
            D((n,)), D((n,)), D((n, 3)), D((n, 3)), D((n, 3)), D((n, 3)),
            D((UNITS,)), D(()), D(()), D((UNITS,)),
            D((n, 3)), D((n, 3)), D((n, 3)), D((n, 3)), D((n,)), D((n,)),
        ],
        compiler_params=pltpu.CompilerParams(collective_id=cid, has_side_effects=True, vmem_limit_bytes=40 << 20),
    )(a)


def padded_2(array, sides, width):
    for axis, dim in sides:
        size, length = (lax.axis_size(axis), array.shape[dim])
        up = [(i, (i + 1) % size) for i in range(size - 1)]
        down = [(j, i) for i, j in up]
        last = lax.slice_in_dim(array, length - width, length, axis=dim)
        initial = lax.slice_in_dim(array, 0, width, axis=dim)
        before = lax.ppermute(last, axis, up)
        after = lax.ppermute(initial, axis, down)
        array = jnp.concatenate([before, array, after], axis=dim)
    return array


def from_partner(block, axis, bit):
    count = lax.axis_size(axis)
    route = []
    for low in range(count):
        high = low | 1 << bit
        if high != low and high < count:
            route += [(low, high), (high, low)]
    return lax.ppermute(block, axis, route)


def silu_slope(values):
    sigma = jax.nn.sigmoid(values)
    return sigma * (1.0 + values * (1.0 - sigma))


def conv_forward(padded, kernel, row_count, col_count):
    total = jnp.zeros((row_count * col_count, kernel.shape[3]), jnp.float32)
    for row_tap in range(3):
        for col_tap in range(3):
            piece = padded[row_tap : row_tap + row_count, col_tap : col_tap + col_count].reshape(
                row_count * col_count, padded.shape[2]
            )
            total = total + jnp.dot(
                piece, kernel[row_tap, col_tap], preferred_element_type=jnp.float32
            )
    return total


def conv_slopes(padded, slope, row_count, col_count):
    pieces = []
    for row_tap in range(3):
        for col_tap in range(3):
            piece = padded[row_tap : row_tap + row_count, col_tap : col_tap + col_count].reshape(
                row_count * col_count, padded.shape[2]
            )
            pieces.append(jnp.einsum("pc,pd->cd", piece, slope, preferred_element_type=jnp.float32))
    return jnp.stack(pieces).reshape(3, 3, padded.shape[2], slope.shape[1])


def conv_back(padded, kernel, row_count, col_count):
    total = jnp.zeros((row_count * col_count, kernel.shape[2]), jnp.float32)
    for row_tap in range(3):
        for col_tap in range(3):
            piece = padded[
                2 - row_tap : 2 - row_tap + row_count, 2 - col_tap : 2 - col_tap + col_count
            ].reshape(row_count * col_count, padded.shape[2])
            total = total + jnp.einsum(
                "pd,cd->pc", piece, kernel[row_tap, col_tap], preferred_element_type=jnp.float32
            )
    return total


def first_forward(tile, first_kernel):
    row_count, col_count, channels = tile.shape
    padded = padded_2(tile, (("gy", 0), ("gx", 1)), 1)
    before = conv_forward(padded, first_kernel, row_count, col_count)
    hidden = jax.nn.silu(before).astype(jnp.bfloat16).reshape(row_count, col_count, channels)
    pooled = (
        hidden.astype(jnp.float32)
        .reshape(row_count // 2, 2, col_count // 2, 2, channels)
        .sum(axis=(1, 3))
        * 0.25
    ).astype(jnp.bfloat16)
    return (padded, before, pooled)


def project(pooled, projection):
    half_rows, half_cols, channels = pooled.shape
    flat = jnp.dot(
        pooled.reshape(half_rows * half_cols, channels),
        projection,
        preferred_element_type=jnp.float32,
    )
    return flat.astype(jnp.bfloat16).reshape(half_rows, half_cols, projection.shape[1])


def second_pass(middle, second_kernel, upstream):
    half_rows, half_cols, wide = middle.shape
    padded = padded_2(middle, (("gy", 0), ("gx", 1)), 1)
    before = conv_forward(padded, second_kernel, half_rows, half_cols)
    output = jax.nn.silu(before).astype(jnp.bfloat16).reshape(half_rows, half_cols, wide)
    flat_up = upstream.reshape(half_rows * half_cols, wide).astype(jnp.float32)
    slope = (flat_up * silu_slope(before)).astype(jnp.bfloat16)
    kernel_grad = conv_slopes(padded, slope, half_rows, half_cols)
    slope_padded = padded_2(slope.reshape(half_rows, half_cols, wide), (("gy", 0), ("gx", 1)), 1)
    back = conv_back(slope_padded, second_kernel, half_rows, half_cols).astype(jnp.bfloat16)
    return (output, kernel_grad, back.reshape(half_rows, half_cols, wide))


def projection_back(pooled, back, projection):
    half_rows, half_cols, channels = pooled.shape
    flat_pool = pooled.reshape(half_rows * half_cols, channels)
    flat_back = back.reshape(half_rows * half_cols, back.shape[2])
    grad = jnp.einsum("pc,pd->cd", flat_pool, flat_back, preferred_element_type=jnp.float32)
    pooled_slope = jnp.einsum(
        "pd,cd->pc", flat_back, projection, preferred_element_type=jnp.float32
    )
    return (grad, pooled_slope.astype(jnp.bfloat16).reshape(half_rows, half_cols, channels))


def first_back(padded, before, pooled_slope):
    half_rows, half_cols, channels = pooled_slope.shape
    spread = jnp.broadcast_to(
        (pooled_slope.astype(jnp.float32) * 0.25)[:, None, :, None, :],
        (half_rows, 2, half_cols, 2, channels),
    )
    spread = spread.reshape(4 * half_rows * half_cols, channels)
    slope = (spread * silu_slope(before)).astype(jnp.bfloat16)
    return conv_slopes(padded, slope, 2 * half_rows, 2 * half_cols)


def per_device(images, first_kernel, projection, second_kernel, cotangent):
    padded, before, pooled = first_forward(images[0], first_kernel)
    middle = from_partner(project(pooled, projection), "section", 0)
    output, grad_second, back_far = second_pass(middle, second_kernel, cotangent[0])
    back = from_partner(back_far, "section", 0)
    grad_projection, pooled_slope = projection_back(pooled, back, projection)
    grad_first = first_back(padded, before, pooled_slope)
    blocks = jnp.concatenate(
        [
            grad_first.reshape(9, 128, 128),
            jnp.zeros((1, 128, 128), jnp.float32),
            grad_projection[None, :, :128],
            grad_projection[None, :, 128:],
        ]
    )
    small = blocks.reshape(3, 2, 2, 128, 128).transpose(0, 1, 3, 2, 4).reshape(3, 256, 256)
    packed = jnp.concatenate([grad_second.reshape(9, 256, 256), small]).astype(jnp.bfloat16)
    total = ar(packed, ((0, 6, True), (6, 6, False)))
    grad_second = total[:9].reshape(3, 3, 256, 256).astype(jnp.float32)
    blocks = total[9:].reshape(3, 2, 128, 2, 128).transpose(0, 1, 3, 2, 4).reshape(12, 128, 128)
    blocks = blocks.astype(jnp.float32)
    grad_first = blocks[:9].reshape(3, 3, 128, 128)
    grad_projection = jnp.concatenate([blocks[10], blocks[11]], axis=1)
    return (output[None], grad_first, grad_projection, grad_second)


def solution(mesh):
    placed = (P("section", "gy", "gx", None), P(), P(), P(), P("section", "gy", "gx", None))
    return jax.shard_map(
        per_device,
        mesh=mesh,
        in_specs=placed,
        out_specs=(P("section", "gy", "gx", None), P(), P(), P()),
        check_vma=False,
    )
```

```python
import functools

import jax
import jax.numpy as jnp
from jax import lax
from jax.experimental import pallas as pl
from jax.experimental.pallas import tpu as pltpu
from jax.sharding import PartitionSpec as P

MESH = pl.DeviceIdType.MESH
F32, BF16 = jnp.float32, jnp.bfloat16
UNITS = 12
CHUNKS = ((0, 5, True), (5, 4, False), (9, 1, True), (10, 2, False))
AROUND = ((-1, 0), (1, 0), (0, -1), (0, 1), (-1, -1), (-1, 1), (1, -1), (1, 1))


def coords():
    s, g, z = lax.axis_index("section"), lax.axis_index("gy"), lax.axis_index("gx")
    core = lax.rem(g, 2)
    x = s * 2 + lax.rem(lax.div(g, 2), 2)
    return x, lax.div(g, 4), core, z


def dev(x, y, core, z):
    return (lax.div(x, 2), y * 4 + lax.rem(x, 2) * 2 + core, z)


def mod4(v):
    return lax.rem(v, 4)


def dot(left, right, dims=((1,), (0,))):
    return lax.dot_general(left, right, (dims, ((), ())), preferred_element_type=F32)


def sigmoid(v):
    return 0.5 * jnp.tanh(0.5 * v) + 0.5


def network(
    img, k1, proj, k2, cot, out, feat,
    xf, xs, w1, d1, pool, mf, m3, cotf, sf, si, s3, ms, s1, fb, pack,
    colpack, rows_in, cols_in, corners_in, cotpack, cot_in, cot_rows, cot_cols,
    r0, h0, r1, h1, r2, h2, zb,
    hs, hr, cs, cr, fs, fr,
    s0s, s0r, s1s, s1r, s2s, s2r, zs, zr, gzs, gzr, g2s, g2r, g1s, g1r, g0s, g0r,
):
    x, y, core, z = coords()
    sec, gy = lax.axis_index("section"), lax.axis_index("gy")
    other_sec = 1 - sec
    sib = dev(x, y, 1 - core, z)

    def near(s, dy, dx):
        return (s, lax.rem(gy + dy + 16, 16), lax.rem(z + dx + 16, 16))

    barrier = pltpu.get_barrier_semaphore()

    def greet(to):
        pl.semaphore_signal(barrier, inc=1, device_id=to, device_id_type=MESH)

    for dy, dx in AROUND:
        greet(near(sec, dy, dx))
        greet(near(other_sec, dy, dx))
    greet(near(other_sec, 0, 0))
    greet(sib)
    for d in range(1, 4):
        greet(dev(mod4(x + d), y, core, z))
        greet(dev(x, mod4(y + d), core, z))
    for d in range(1, 16):
        greet(dev(x, y, core, lax.rem(z + d, 16)))

    xf[5:37, 24:88] = img[...].astype(F32)
    colpack[0] = xf[5:37, 24:32].reshape(256, 128).astype(BF16)
    colpack[1] = xf[5:37, 80:88].reshape(256, 128).astype(BF16)
    cotf[0:16, 0:32] = cot[...].astype(F32)
    cotpack[0] = cotf[0:16, 0, :].astype(BF16)
    cotpack[1] = cotf[0:16, 31, :].astype(BF16)

    pl.semaphore_wait(barrier, 39)
    sends = []

    def push(src, dst, ss, rs, to):
        c = pltpu.make_async_remote_copy(
            src_ref=src, dst_ref=dst, send_sem=ss, recv_sem=rs, device_id=to, device_id_type=MESH
        )
        c.start()
        sends.append(c)
        return c

    halo = [
        push(img.at[0:5], rows_in.at[1], hs.at[0], hr.at[0], near(sec, -1, 0)),
        push(img.at[27:32], rows_in.at[0], hs.at[1], hr.at[1], near(sec, 1, 0)),
        push(colpack.at[0], cols_in.at[1], hs.at[2], hr.at[2], near(sec, 0, -1)),
        push(colpack.at[1], cols_in.at[0], hs.at[3], hr.at[3], near(sec, 0, 1)),
        push(colpack.at[0, 0:48], corners_in.at[3], hs.at[4], hr.at[4], near(sec, -1, -1)),
        push(colpack.at[1, 0:48], corners_in.at[2], hs.at[5], hr.at[5], near(sec, -1, 1)),
        push(colpack.at[0, 208:256], corners_in.at[1], hs.at[6], hr.at[6], near(sec, 1, -1)),
        push(colpack.at[1, 208:256], corners_in.at[0], hs.at[7], hr.at[7], near(sec, 1, 1)),
    ]
    cots = [
        push(cot, cot_in, cs.at[0], cr.at[0], near(other_sec, 0, 0)),
        push(cot.at[0], cot_rows.at[1], cs.at[1], cr.at[1], near(other_sec, -1, 0)),
        push(cot.at[15], cot_rows.at[0], cs.at[2], cr.at[2], near(other_sec, 1, 0)),
        push(cotpack.at[0], cot_cols.at[1, 1], cs.at[3], cr.at[3], near(other_sec, 0, -1)),
        push(cotpack.at[1], cot_cols.at[0, 1], cs.at[4], cr.at[4], near(other_sec, 0, 1)),
        push(cotpack.at[0], cot_cols.at[1, 2], cs.at[5], cr.at[5], near(other_sec, -1, -1)),
        push(cotpack.at[1], cot_cols.at[0, 2], cs.at[6], cr.at[6], near(other_sec, -1, 1)),
        push(cotpack.at[0], cot_cols.at[1, 0], cs.at[7], cr.at[7], near(other_sec, 1, -1)),
        push(cotpack.at[1], cot_cols.at[0, 0], cs.at[8], cr.at[8], near(other_sec, 1, 1)),
    ]

    zero = jnp.zeros((128, 128), BF16)
    for a in range(3):
        w1[a, 384:512, 0:128] = zero
        w1[a, 0:128, 128:256] = zero
        for b in range(3):
            w1[a, b * 128 : b * 128 + 128, 0:128] = k1[a, b]
            w1[a, b * 128 + 128 : b * 128 + 256, 128:256] = k1[a, b]
    xf[:, 0:16] = jnp.zeros((42, 16, 128), F32)
    xf[:, 96:112] = jnp.zeros((42, 16, 128), F32)
    mf[:, 0:8] = jnp.zeros((20, 8, 256), F32)
    mf[:, 56:64] = jnp.zeros((20, 8, 256), F32)
    cotf[...] = jnp.zeros((18, 48, 256), F32)

    for c in halo:
        c.wait_recv()
    xf[0:5, 24:88] = rows_in[0].astype(F32)
    xf[37:42, 24:88] = rows_in[1].astype(F32)
    for side, at in ((0, 16), (1, 88)):
        xf[5:37, at : at + 8] = cols_in[side].astype(F32).reshape(32, 8, 128)
        xf[0:5, at : at + 8] = corners_in[side].astype(F32).reshape(6, 8, 128)[1:6]
        xf[37:42, at : at + 8] = corners_in[2 + side].astype(F32).reshape(6, 8, 128)[0:5]

    @pl.when(gy == 0)
    def _():
        xf[0:5, 16:96] = jnp.zeros((5, 80, 128), F32)

    @pl.when(gy == 15)
    def _():
        xf[37:42, 16:96] = jnp.zeros((5, 80, 128), F32)

    @pl.when(z == 0)
    def _():
        xf[:, 16:24] = jnp.zeros((42, 8, 128), F32)

    @pl.when(z == 15)
    def _():
        xf[:, 88:96] = jnp.zeros((42, 8, 128), F32)

    @pl.loop(0, 21)
    def _(t):
        rs = pl.ds(t * 2, 2)
        for p in range(4):
            lanes = slice(p * 128, p * 128 + 128)
            xs[rs, 0:32, lanes] = xf[rs, pl.ds(23 + p, 32, 2), :].astype(BF16)
            right = xf[rs, pl.ds(87 + p, 8, 2), :]
            left = xf[rs, pl.ds(7 + p, 8, 2), :]
            xs[rs, 32:48, lanes] = jnp.concatenate([right, left], axis=1).astype(BF16)

    @pl.loop(0, 5)
    def _(t):
        acc = dot(xs[pl.ds(t * 8, 8)].reshape(384, 512), w1[0])
        acc += dot(xs[pl.ds(t * 8 + 1, 8)].reshape(384, 512), w1[1])
        acc += dot(xs[pl.ds(t * 8 + 2, 8)].reshape(384, 512), w1[2])
        sig = sigmoid(acc)
        hid = (acc * sig).astype(BF16).astype(F32).reshape(4, 2, 48, 256)
        slope = sig * (1.0 + acc * (1.0 - sig))
        d1[pl.ds(t * 8, 8)] = slope.reshape(8, 48, 256)[:, 0:32]
        total = hid[:, 0] + hid[:, 1]
        total = (total[:, :, 0:128] + total[:, :, 128:256]) * 0.25
        row = lax.broadcasted_iota(jnp.int32, (4, 48, 128), 0) + (t * 4 - 2 + gy * 16)
        k = lax.broadcasted_iota(jnp.int32, (4, 48, 128), 1)
        col = jnp.where(k < 40, k, k - 48) + z * 32
        inside = (row >= 0) & (row < 256) & (col >= 0) & (col < 512)
        pooled = jnp.where(inside, total, 0.0).astype(BF16)
        pool[pl.ds(t * 4, 4)] = pooled[:, 0:32]
        mid = dot(pooled.reshape(192, 128), proj[...]).astype(BF16).astype(F32).reshape(4, 48, 256)
        mf[pl.ds(t * 4, 4), 16:56] = mid[:, 0:40]
        mf[pl.ds(t * 4, 4), 8:16] = mid[:, 40:48]

    @pl.loop(0, 10)
    def _(t):
        rs = pl.ds(t * 2, 2)
        for b in range(3):
            lanes = slice(b * 256, b * 256 + 256)
            m3[rs, 0:32, lanes] = mf[rs, 15 + b : 47 + b, :].astype(BF16)
            sides = [mf[rs, 47 + b : 55 + b, :], mf[rs, 7 + b : 15 + b, :]]
            m3[rs, 32:48, lanes] = jnp.concatenate(sides, axis=1).astype(BF16)

    for c in cots:
        c.wait_recv()
    cotf[1:17, 0:32] = cot_in[...].astype(F32)
    cotf[0, 0:32] = cot_rows[0].astype(F32)
    cotf[17, 0:32] = cot_rows[1].astype(F32)
    for side, at in ((0, 47), (1, 32)):
        column = cot_cols[side, 1].astype(F32)
        for q in range(16):
            cotf[1 + q, at : at + 1, :] = column[q : q + 1]
        cotf[0, at : at + 1, :] = cot_cols[side, 0].astype(F32)[15:16]
        cotf[17, at : at + 1, :] = cot_cols[side, 2].astype(F32)[0:1]

    @pl.when(gy == 0)
    def _():
        cotf[0] = jnp.zeros((48, 256), F32)

    @pl.when(gy == 15)
    def _():
        cotf[17] = jnp.zeros((48, 256), F32)

    @pl.when(z == 0)
    def _():
        cotf[:, 40:48] = jnp.zeros((18, 8, 256), F32)

    @pl.when(z == 15)
    def _():
        cotf[:, 32:40] = jnp.zeros((18, 8, 256), F32)

    @pl.loop(0, 3)
    def _(t):
        acc = dot(m3[pl.ds(t * 6, 6)].reshape(288, 768), k2[0].reshape(768, 256))
        acc += dot(m3[pl.ds(t * 6 + 1, 6)].reshape(288, 768), k2[1].reshape(768, 256))
        acc += dot(m3[pl.ds(t * 6 + 2, 6)].reshape(288, 768), k2[2].reshape(768, 256))
        sig = sigmoid(acc)
        fb[pl.ds(t * 6, 6)] = (acc * sig).astype(BF16).reshape(6, 48, 256)[:, 0:32]
        slope = (sig * (1.0 + acc * (1.0 - sig))).reshape(6, 48, 256) * cotf[pl.ds(t * 6, 6)]
        slope = slope.astype(BF16)
        si[pl.ds(t * 6, 6)] = slope[:, 0:32]
        slope = slope.astype(F32)
        sf[pl.ds(t * 6, 6), 16:56] = slope[:, 0:40]
        sf[pl.ds(t * 6, 6), 8:16] = slope[:, 40:48]

    feat_copy = push(fb.at[1:17], feat, fs, fr, near(other_sec, 0, 0))

    for a in range(3):
        grad = dot(m3[a + 1 : a + 17, 0:32].reshape(512, 768), si[1:17].reshape(512, 256), ((0,), (0,)))
        pack[3 * a : 3 * a + 3] = grad.reshape(3, 256, 256).astype(BF16)

    mine = pl.ds(pl.multiple_of(core * 128, 128), 128)
    other = pl.ds(pl.multiple_of((1 - core) * 128, 128), 128)

    def axes(yfirst):
        if yfirst:
            return (y, lambda p: dev(x, p, core, z)), (x, lambda p: dev(p, y, core, z))
        return (x, lambda p: dev(p, y, core, z)), (y, lambda p: dev(x, p, core, z))

    def st0(ci):
        u0, n, yf = CHUNKS[ci]
        us = pl.ds(u0, n)
        return [push(pack.at[us, :, other], r0.at[us], s0s.at[ci], s0r.at[ci], sib)]

    def st1(ci, c):
        u0, n, yf = CHUNKS[ci]
        us = pl.ds(u0, n)
        c[0].wait_recv()
        h0[us] = (pack[us, :, mine].astype(F32) + r0[us].astype(F32)).astype(BF16)
        (fm, fd), _ = axes(yf)
        out_c = []
        for d in range(1, 4):
            p = mod4(fm + d)
            out_c.append(push(h0.at[us, pl.ds(pl.multiple_of(p * 64, 64), 64)], r1.at[d - 1, us], s1s.at[ci, d - 1], s1r.at[ci, d - 1], fd(p)))
        return out_c

    def st2(ci, c):
        u0, n, yf = CHUNKS[ci]
        us = pl.ds(u0, n)
        for k in c:
            k.wait_recv()
        (fm, fd), (sm, sd) = axes(yf)
        h1[us] = (h0[us, pl.ds(pl.multiple_of(fm * 64, 64), 64)].astype(F32) + r1[0, us].astype(F32) + r1[1, us].astype(F32) + r1[2, us].astype(F32)).astype(BF16)
        out_c = []
        for d in range(1, 4):
            p = mod4(sm + d)
            out_c.append(push(h1.at[us, pl.ds(pl.multiple_of(p * 16, 16), 16)], r2.at[d - 1, us], s2s.at[ci, d - 1], s2r.at[ci, d - 1], sd(p)))
        return out_c

    def st3(ci, c):
        u0, n, yf = CHUNKS[ci]
        us = pl.ds(u0, n)
        for k in c:
            k.wait_recv()
        (fm, fd), (sm, sd) = axes(yf)
        h2[us] = (h1[us, pl.ds(pl.multiple_of(sm * 16, 16), 16)].astype(F32) + r2[0, us].astype(F32) + r2[1, us].astype(F32) + r2[2, us].astype(F32)).astype(BF16)
        for u in range(u0, u0 + n):
            @pl.when(z != u)
            def _():
                pltpu.make_async_remote_copy(src_ref=h2.at[u], dst_ref=zb.at[z], send_sem=zs.at[u], recv_sem=zr.at[ci // 2], device_id=dev(x, y, core, u), device_id_type=MESH).start()
        return None

    def rows16(yf):
        (fm, fd), (sm, sd) = axes(yf)
        return pl.ds(pl.multiple_of(fm * 64 + sm * 16, 16), 16)

    def rows64(yf):
        (fm, fd), (sm, sd) = axes(yf)
        return pl.ds(pl.multiple_of(fm * 64, 64), 64)

    def st4(ci, c):
        u0, n, yf = CHUNKS[ci]
        r16 = rows16(yf)
        @pl.when(jnp.logical_and(z >= u0, z < u0 + n))
        def _():
            zb[z] = h2[z]
            pltpu.make_async_copy(zb.at[pl.ds(0, 15)], zb.at[pl.ds(0, 15)], zr.at[ci // 2]).wait()
            tot = zb[0].astype(F32)
            for k in range(1, 16):
                tot = tot + zb[k].astype(F32)
            out[z, r16, mine] = tot.astype(BF16)
            for d in range(1, 16):
                to = lax.rem(z + d, 16)
                pltpu.make_async_remote_copy(src_ref=out.at[z, r16, mine], dst_ref=out.at[z, r16, mine], send_sem=gzs.at[ci // 2], recv_sem=gzr.at[z], device_id=dev(x, y, core, to), device_id_type=MESH).start()
        return None

    def st5(ci, c):
        u0, n, yf = CHUNKS[ci]
        us = pl.ds(u0, n)
        r16 = rows16(yf)
        for u in range(u0, u0 + n):
            @pl.when(z != u)
            def _():
                pltpu.make_async_copy(out.at[u, r16, mine], out.at[u, r16, mine], gzr.at[u]).wait()
        (fm, fd), (sm, sd) = axes(yf)
        return [push(out.at[us, r16, mine], out.at[us, r16, mine], g2s.at[ci, d - 1], g2r.at[ci, d - 1], sd(mod4(sm + d))) for d in range(1, 4)]

    def st6(ci, c):
        u0, n, yf = CHUNKS[ci]
        us = pl.ds(u0, n)
        for k in c:
            k.wait_recv()
        r64 = rows64(yf)
        (fm, fd), (sm, sd) = axes(yf)
        return [push(out.at[us, r64, mine], out.at[us, r64, mine], g1s.at[ci, d - 1], g1r.at[ci, d - 1], fd(mod4(fm + d))) for d in range(1, 4)]

    def st7(ci, c):
        u0, n, yf = CHUNKS[ci]
        us = pl.ds(u0, n)
        for k in c:
            k.wait_recv()
        return [push(out.at[us, :, mine], out.at[us, :, mine], g0s.at[ci], g0r.at[ci], sib)]


    state = [st0(0), st0(1), None, None]

    @pl.loop(0, 9)
    def _(t):
        rs = pl.ds(t * 2, 2)
        for b in range(3):
            s3[rs, :, b * 256 : b * 256 + 256] = sf[rs, 17 - b : 49 - b, :].astype(BF16)

    @pl.loop(0, 2)
    def _(t):
        acc = jnp.zeros((256, 256), F32)
        for a in range(3):
            for b in range(3):
                piece = s3[pl.ds(t * 8 + 2 - a, 8), :, b * 256 : b * 256 + 256].reshape(256, 256)
                acc += dot(piece, k2[a, b], ((1,), (1,)))
        ms[pl.ds(pl.multiple_of(t * 256, 256), 256)] = acc.astype(BF16)

    state[0] = st1(0, state[0])
    state[1] = st1(1, state[1])

    pack[11, 128:256, :] = dot(pool[2:18].reshape(512, 128), ms[...], ((0,), (0,))).astype(BF16)
    pack[11, 0:128, 128:256] = jnp.zeros((128, 128), BF16)

    @pl.loop(0, 4)
    def _(t):
        part = ms[pl.ds(pl.multiple_of(t * 128, 128), 128)]
        back = dot(part, proj[...], ((1,), (1,))).astype(BF16).astype(F32) * 0.25
        back = back.reshape(4, 32, 128)
        back = jnp.concatenate([back, back], axis=2)
        slope = d1[pl.ds(t * 8 + 4, 8)].reshape(4, 2, 32, 256)
        slope = jnp.stack([slope[:, 0] * back, slope[:, 1] * back], axis=1)
        s1[pl.ds(t * 8, 8)] = slope.reshape(8, 32, 256).astype(BF16)

    for a in range(3):
        grad = dot(xs[a + 4 : a + 36, 0:32].reshape(1024, 512), s1[...].reshape(1024, 256), ((0,), (0,)))
        for b in range(3):
            t = 3 * a + b
            tap = grad[b * 128 : b * 128 + 128, 0:128] + grad[b * 128 + 128 : b * 128 + 256, 128:256]
            pack[
                9 + t // 4, (t // 2) % 2 * 128 : (t // 2) % 2 * 128 + 128, t % 2 * 128 : t % 2 * 128 + 128
            ] = tap.astype(BF16)

    state[2], state[3] = st0(2), st0(3)
    state[0] = st2(0, state[0])
    state[1] = st2(1, state[1])
    state[2] = st1(2, state[2])
    state[3] = st1(3, state[3])
    for ci in range(4):
        state[ci] = (st3 if ci < 2 else st2)(ci, state[ci])
    for ci in range(4):
        state[ci] = (st4 if ci < 2 else st3)(ci, state[ci])
    for ci in range(4):
        state[ci] = (st5 if ci < 2 else st4)(ci, state[ci])
    for ci in range(4):
        state[ci] = (st6 if ci < 2 else st5)(ci, state[ci])
    for ci in range(4):
        state[ci] = (st7 if ci < 2 else st6)(ci, state[ci])
    for ci in (2, 3):
        state[ci] = st7(ci, state[ci])
    for c in state:
        for e in c:
            e.wait_recv()
    feat_copy.wait_recv()
    for c in sends:
        c.wait_send()
    for u in range(UNITS):
        @pl.when(z != u)
        def _():
            pltpu.make_async_copy(h2.at[u], h2.at[u], zs.at[u]).wait()
    for half, (lo, hi) in enumerate(((0, 9), (9, 12))):
        @pl.when(jnp.logical_and(z >= lo, z < hi))
        def _():
            pltpu.make_async_copy(zb.at[pl.ds(0, 15)], zb.at[pl.ds(0, 15)], gzs.at[half]).wait()


def network_call(img, k1, proj, k2, cot):
    V, D = pltpu.VMEM, pltpu.SemaphoreType.DMA
    n = len(CHUNKS)
    macs = 2 * 1000 * 1000 * 1000
    return pl.pallas_call(
        network,
        out_shape=(
            jax.ShapeDtypeStruct((UNITS, 256, 256), BF16),
            jax.ShapeDtypeStruct((16, 32, 256), BF16),
        ),
        in_specs=[pl.BlockSpec(memory_space=pltpu.VMEM)] * 5,
        out_specs=(pl.BlockSpec(memory_space=pltpu.VMEM),) * 2,
        scratch_shapes=[
            V((42, 112, 128), F32), V((42, 48, 512), BF16), V((3, 512, 256), BF16),
            V((40, 32, 256), F32), V((20, 32, 128), BF16), V((20, 64, 256), F32),
            V((20, 48, 768), BF16), V((18, 48, 256), F32), V((18, 64, 256), F32),
            V((18, 32, 256), BF16), V((18, 32, 768), BF16), V((512, 256), BF16),
            V((32, 32, 256), BF16), V((18, 32, 256), BF16), V((UNITS, 256, 256), BF16),
            V((2, 256, 128), BF16), V((2, 5, 64, 128), BF16), V((2, 256, 128), BF16),
            V((4, 48, 128), BF16), V((2, 16, 256), BF16), V((16, 32, 256), BF16),
            V((2, 32, 256), BF16), V((2, 3, 16, 256), BF16),
            V((UNITS, 256, 128), BF16), V((UNITS, 256, 128), BF16),
            V((3, UNITS, 64, 128), BF16), V((UNITS, 64, 128), BF16),
            V((3, UNITS, 16, 128), BF16), V((UNITS, 16, 128), BF16), V((16, 16, 128), BF16),
            D((8,)), D((8,)), D((9,)), D((9,)), D(()), D(()),
            D((n,)), D((n,)), D((n, 3)), D((n, 3)), D((n, 3)), D((n, 3)),
            D((UNITS,)), D((2,)), D((2,)), D((UNITS,)),
            D((n, 3)), D((n, 3)), D((n, 3)), D((n, 3)), D((n,)), D((n,)),
        ],
        compiler_params=pltpu.CompilerParams(
            collective_id=0, has_side_effects=True, vmem_limit_bytes=56 << 20
        ),
        cost_estimate=pl.CostEstimate(
            flops=2 * macs, bytes_accessed=8 << 20, transcendentals=1 << 20
        ),
    )(img, k1, proj, k2, cot)


def per_device(images, first_kernel, projection, second_kernel, cotangent):
    total, features = network_call(images[0], first_kernel, projection, second_kernel, cotangent[0])
    grad_second = total[:9].reshape(3, 3, 256, 256).astype(F32)
    blocks = total[9:].reshape(3, 2, 128, 2, 128).transpose(0, 1, 3, 2, 4).reshape(12, 128, 128)
    blocks = blocks.astype(F32)
    grad_first = blocks[:9].reshape(3, 3, 128, 128)
    grad_projection = jnp.concatenate([blocks[10], blocks[11]], axis=1)
    return (features[None], grad_first, grad_projection, grad_second)


def solution(mesh):
    placed = (P("section", "gy", "gx", None), P(), P(), P(), P("section", "gy", "gx", None))
    return jax.shard_map(
        per_device,
        mesh=mesh,
        in_specs=placed,
        out_specs=(P("section", "gy", "gx", None), P(), P(), P()),
        check_vma=False,
    )
```

```python
import functools

import jax
import jax.numpy as jnp
from jax import lax
from jax.experimental import pallas as pl
from jax.experimental.pallas import tpu as pltpu
from jax.sharding import PartitionSpec as P

MESH = pl.DeviceIdType.MESH
F32, BF16 = jnp.float32, jnp.bfloat16
UNITS = 12
CHUNKS = ((0, 4, True), (4, 4, False), (8, 2, True), (10, 2, False))
AROUND = ((-1, 0), (1, 0), (0, -1), (0, 1), (-1, -1), (-1, 1), (1, -1), (1, 1))


def coords():
    s, g, z = lax.axis_index("section"), lax.axis_index("gy"), lax.axis_index("gx")
    core = lax.rem(g, 2)
    x = s * 2 + lax.rem(lax.div(g, 2), 2)
    return x, lax.div(g, 4), core, z


def dev(x, y, core, z):
    return (lax.div(x, 2), y * 4 + lax.rem(x, 2) * 2 + core, z)


def mod4(v):
    return lax.rem(v, 4)


def dot(left, right, dims=((1,), (0,))):
    return lax.dot_general(left, right, (dims, ((), ())), preferred_element_type=F32)


def sigmoid(v):
    return 0.5 * jnp.tanh(0.5 * v) + 0.5


def network(
    img_in, k1_in, proj_in, k2_in, cot_h, out, feat,
    img, k1, proj, k2, cot, fetch,
    xf, xs, w1, d1, pool, mf, m3, cotf, sf, si, s3, ms, s1, fb, pack,
    colpack, rows_in, cols_in, corners_in, cotpack, cot_in, cot_rows, cot_cols,
    r0, h0, r1, h1, r2, h2, ra, hz, rb0, rl, rb1,
    hs, hr, cs, cr, fs, fr,
    s0s, s0r, s1s, s1r, s2s, s2r, zas, zar, zbs, zbr, zcs, zcr, g2s, g2r, g1s, g1r, g0s, g0r, ready,
):
    x, y, core, z = coords()
    sec, gy = lax.axis_index("section"), lax.axis_index("gy")
    other_sec = 1 - sec
    sib = dev(x, y, 1 - core, z)

    def near(s, dy, dx):
        return (s, lax.rem(gy + dy + 16, 16), lax.rem(z + dx + 16, 16))

    barrier = pltpu.get_barrier_semaphore()

    def greet(to):
        pl.semaphore_signal(barrier, inc=1, device_id=to, device_id_type=MESH)

    for dy, dx in AROUND:
        greet(near(sec, dy, dx))
        greet(near(other_sec, dy, dx))
    greet(near(other_sec, 0, 0))
    greet(sib)
    for d in range(1, 4):
        greet(dev(mod4(x + d), y, core, z))
        greet(dev(x, mod4(y + d), core, z))
    zl, zh = mod4(z), lax.div(z, 4)
    for d in range(1, 4):
        greet(dev(x, y, core, zh * 4 + mod4(zl + d)))
    greet(dev(x, y, core, lax.rem(z + 4, 16)))
    greet(dev(x, y, core, lax.rem(z + 12, 16)))

    fetches = [
        pltpu.make_async_copy(src, dst, fetch.at[i])
        for i, (src, dst) in enumerate(
            ((img_in, img), (cot_h, cot), (k1_in, k1), (proj_in, proj), (k2_in, k2))
        )
    ]
    for c in fetches:
        c.start()
    fetches[0].wait()
    xf[5:37, 24:88] = img[...].astype(F32)
    colpack[0] = xf[5:37, 24:32].reshape(256, 128).astype(BF16)
    colpack[1] = xf[5:37, 80:88].reshape(256, 128).astype(BF16)
    fetches[1].wait()
    cotf[0:16, 0:32] = cot[...].astype(F32)
    cotpack[0] = cotf[0:16, 0, :].astype(BF16)
    cotpack[1] = cotf[0:16, 31, :].astype(BF16)

    pl.semaphore_wait(barrier, 29)
    pl.semaphore_signal(
        ready, inc=1, device_id=dev(x, y, core, lax.rem(z + 12, 16)), device_id_type=MESH
    )
    sends = []

    def push(src, dst, ss, rs, to):
        c = pltpu.make_async_remote_copy(
            src_ref=src, dst_ref=dst, send_sem=ss, recv_sem=rs, device_id=to, device_id_type=MESH
        )
        c.start()
        sends.append(c)
        return c

    halo = [
        push(img.at[0:5], rows_in.at[1], hs.at[0], hr.at[0], near(sec, -1, 0)),
        push(img.at[27:32], rows_in.at[0], hs.at[1], hr.at[1], near(sec, 1, 0)),
        push(colpack.at[0], cols_in.at[1], hs.at[2], hr.at[2], near(sec, 0, -1)),
        push(colpack.at[1], cols_in.at[0], hs.at[3], hr.at[3], near(sec, 0, 1)),
        push(colpack.at[0, 0:48], corners_in.at[3], hs.at[4], hr.at[4], near(sec, -1, -1)),
        push(colpack.at[1, 0:48], corners_in.at[2], hs.at[5], hr.at[5], near(sec, -1, 1)),
        push(colpack.at[0, 208:256], corners_in.at[1], hs.at[6], hr.at[6], near(sec, 1, -1)),
        push(colpack.at[1, 208:256], corners_in.at[0], hs.at[7], hr.at[7], near(sec, 1, 1)),
    ]
    cots = [
        push(cot, cot_in, cs.at[0], cr.at[0], near(other_sec, 0, 0)),
        push(cot.at[0], cot_rows.at[1], cs.at[1], cr.at[1], near(other_sec, -1, 0)),
        push(cot.at[15], cot_rows.at[0], cs.at[2], cr.at[2], near(other_sec, 1, 0)),
        push(cotpack.at[0], cot_cols.at[1, 1], cs.at[3], cr.at[3], near(other_sec, 0, -1)),
        push(cotpack.at[1], cot_cols.at[0, 1], cs.at[4], cr.at[4], near(other_sec, 0, 1)),
        push(cotpack.at[0], cot_cols.at[1, 2], cs.at[5], cr.at[5], near(other_sec, -1, -1)),
        push(cotpack.at[1], cot_cols.at[0, 2], cs.at[6], cr.at[6], near(other_sec, -1, 1)),
        push(cotpack.at[0], cot_cols.at[1, 0], cs.at[7], cr.at[7], near(other_sec, 1, -1)),
        push(cotpack.at[1], cot_cols.at[0, 0], cs.at[8], cr.at[8], near(other_sec, 1, 1)),
    ]

    fetches[2].wait()
    zero = jnp.zeros((128, 128), BF16)
    for a in range(3):
        w1[a, 384:512, 0:128] = zero
        w1[a, 0:128, 128:256] = zero
        for b in range(3):
            w1[a, b * 128 : b * 128 + 128, 0:128] = k1[a, b]
            w1[a, b * 128 + 128 : b * 128 + 256, 128:256] = k1[a, b]
    xf[:, 0:16] = jnp.zeros((42, 16, 128), F32)
    xf[:, 96:112] = jnp.zeros((42, 16, 128), F32)
    mf[:, 0:8] = jnp.zeros((20, 8, 256), F32)
    mf[:, 56:64] = jnp.zeros((20, 8, 256), F32)
    cotf[...] = jnp.zeros((18, 48, 256), F32)

    fetches[3].wait()
    fetches[4].wait()
    for c in halo:
        c.wait_recv()
    xf[0:5, 24:88] = rows_in[0].astype(F32)
    xf[37:42, 24:88] = rows_in[1].astype(F32)
    for side, at in ((0, 16), (1, 88)):
        xf[5:37, at : at + 8] = cols_in[side].astype(F32).reshape(32, 8, 128)
        xf[0:5, at : at + 8] = corners_in[side].astype(F32).reshape(6, 8, 128)[1:6]
        xf[37:42, at : at + 8] = corners_in[2 + side].astype(F32).reshape(6, 8, 128)[0:5]

    @pl.when(gy == 0)
    def _():
        xf[0:5, 16:96] = jnp.zeros((5, 80, 128), F32)

    @pl.when(gy == 15)
    def _():
        xf[37:42, 16:96] = jnp.zeros((5, 80, 128), F32)

    @pl.when(z == 0)
    def _():
        xf[:, 16:24] = jnp.zeros((42, 8, 128), F32)

    @pl.when(z == 15)
    def _():
        xf[:, 88:96] = jnp.zeros((42, 8, 128), F32)

    @pl.loop(0, 21)
    def _(t):
        rs = pl.ds(t * 2, 2)
        for p in range(4):
            lanes = slice(p * 128, p * 128 + 128)
            xs[rs, 0:32, lanes] = xf[rs, pl.ds(23 + p, 32, 2), :].astype(BF16)
            right = xf[rs, pl.ds(87 + p, 8, 2), :]
            left = xf[rs, pl.ds(7 + p, 8, 2), :]
            xs[rs, 32:48, lanes] = jnp.concatenate([right, left], axis=1).astype(BF16)

    @pl.loop(0, 5)
    def _(t):
        acc = dot(xs[pl.ds(t * 8, 8)].reshape(384, 512), w1[0])
        acc += dot(xs[pl.ds(t * 8 + 1, 8)].reshape(384, 512), w1[1])
        acc += dot(xs[pl.ds(t * 8 + 2, 8)].reshape(384, 512), w1[2])
        sig = sigmoid(acc)
        hid = (acc * sig).astype(BF16).astype(F32).reshape(4, 2, 48, 256)
        slope = sig * (1.0 + acc * (1.0 - sig))
        d1[pl.ds(t * 8, 8)] = slope.reshape(8, 48, 256)[:, 0:32]
        total = hid[:, 0] + hid[:, 1]
        total = (total[:, :, 0:128] + total[:, :, 128:256]) * 0.25
        row = lax.broadcasted_iota(jnp.int32, (4, 48, 128), 0) + (t * 4 - 2 + gy * 16)
        k = lax.broadcasted_iota(jnp.int32, (4, 48, 128), 1)
        col = jnp.where(k < 40, k, k - 48) + z * 32
        inside = (row >= 0) & (row < 256) & (col >= 0) & (col < 512)
        pooled = jnp.where(inside, total, 0.0).astype(BF16)
        pool[pl.ds(t * 4, 4)] = pooled[:, 0:32]
        mid = dot(pooled.reshape(192, 128), proj[...]).astype(BF16).astype(F32).reshape(4, 48, 256)
        mf[pl.ds(t * 4, 4), 16:56] = mid[:, 0:40]
        mf[pl.ds(t * 4, 4), 8:16] = mid[:, 40:48]

    @pl.loop(0, 10)
    def _(t):
        rs = pl.ds(t * 2, 2)
        for b in range(3):
            lanes = slice(b * 256, b * 256 + 256)
            m3[rs, 0:32, lanes] = mf[rs, 15 + b : 47 + b, :].astype(BF16)
            sides = [mf[rs, 47 + b : 55 + b, :], mf[rs, 7 + b : 15 + b, :]]
            m3[rs, 32:48, lanes] = jnp.concatenate(sides, axis=1).astype(BF16)

    for c in cots:
        c.wait_recv()
    cotf[1:17, 0:32] = cot_in[...].astype(F32)
    cotf[0, 0:32] = cot_rows[0].astype(F32)
    cotf[17, 0:32] = cot_rows[1].astype(F32)
    for side, at in ((0, 47), (1, 32)):
        column = cot_cols[side, 1].astype(F32)
        for q in range(16):
            cotf[1 + q, at : at + 1, :] = column[q : q + 1]
        cotf[0, at : at + 1, :] = cot_cols[side, 0].astype(F32)[15:16]
        cotf[17, at : at + 1, :] = cot_cols[side, 2].astype(F32)[0:1]

    @pl.when(gy == 0)
    def _():
        cotf[0] = jnp.zeros((48, 256), F32)

    @pl.when(gy == 15)
    def _():
        cotf[17] = jnp.zeros((48, 256), F32)

    @pl.when(z == 0)
    def _():
        cotf[:, 40:48] = jnp.zeros((18, 8, 256), F32)

    @pl.when(z == 15)
    def _():
        cotf[:, 32:40] = jnp.zeros((18, 8, 256), F32)

    @pl.loop(0, 3)
    def _(t):
        acc = dot(m3[pl.ds(t * 6, 6)].reshape(288, 768), k2[0].reshape(768, 256))
        acc += dot(m3[pl.ds(t * 6 + 1, 6)].reshape(288, 768), k2[1].reshape(768, 256))
        acc += dot(m3[pl.ds(t * 6 + 2, 6)].reshape(288, 768), k2[2].reshape(768, 256))
        sig = sigmoid(acc)
        fb[pl.ds(t * 6, 6)] = (acc * sig).astype(BF16).reshape(6, 48, 256)[:, 0:32]
        slope = (sig * (1.0 + acc * (1.0 - sig))).reshape(6, 48, 256) * cotf[pl.ds(t * 6, 6)]
        slope = slope.astype(BF16)
        si[pl.ds(t * 6, 6)] = slope[:, 0:32]
        slope = slope.astype(F32)
        sf[pl.ds(t * 6, 6), 16:56] = slope[:, 0:40]
        sf[pl.ds(t * 6, 6), 8:16] = slope[:, 40:48]

    feat_copy = push(fb.at[1:17], feat, fs, fr, near(other_sec, 0, 0))

    for a in range(3):
        grad = dot(m3[a + 1 : a + 17, 0:32].reshape(512, 768), si[1:17].reshape(512, 256), ((0,), (0,)))
        pack[3 * a : 3 * a + 3] = grad.reshape(3, 256, 256).astype(BF16)

    mine = pl.ds(pl.multiple_of(core * 128, 128), 128)
    other = pl.ds(pl.multiple_of((1 - core) * 128, 128), 128)

    def axes(yfirst):
        if yfirst:
            return (y, lambda p: dev(x, p, core, z)), (x, lambda p: dev(p, y, core, z))
        return (x, lambda p: dev(p, y, core, z)), (y, lambda p: dev(x, p, core, z))

    def st0(ci):
        u0, n, yf = CHUNKS[ci]
        us = pl.ds(u0, n)
        return [push(pack.at[us, :, other], r0.at[us], s0s.at[ci], s0r.at[ci], sib)]

    def st1(ci, c):
        u0, n, yf = CHUNKS[ci]
        us = pl.ds(u0, n)
        c[0].wait_recv()
        h0[us] = (pack[us, :, mine].astype(F32) + r0[us].astype(F32)).astype(BF16)
        (fm, fd), _ = axes(yf)
        out_c = []
        for d in range(1, 4):
            p = mod4(fm + d)
            out_c.append(push(h0.at[us, pl.ds(pl.multiple_of(p * 64, 64), 64)], r1.at[d - 1, us], s1s.at[ci, d - 1], s1r.at[ci, d - 1], fd(p)))
        return out_c

    def st2(ci, c):
        u0, n, yf = CHUNKS[ci]
        us = pl.ds(u0, n)
        for k in c:
            k.wait_recv()
        (fm, fd), (sm, sd) = axes(yf)
        h1[us] = (h0[us, pl.ds(pl.multiple_of(fm * 64, 64), 64)].astype(F32) + r1[0, us].astype(F32) + r1[1, us].astype(F32) + r1[2, us].astype(F32)).astype(BF16)
        out_c = []
        for d in range(1, 4):
            p = mod4(sm + d)
            out_c.append(push(h1.at[us, pl.ds(pl.multiple_of(p * 16, 16), 16)], r2.at[d - 1, us], s2s.at[ci, d - 1], s2r.at[ci, d - 1], sd(p)))
        return out_c

    def st3(ci, c):
        u0, n, yf = CHUNKS[ci]
        us = pl.ds(u0, n)
        for k in c:
            k.wait_recv()
        (fm, fd), (sm, sd) = axes(yf)
        h2[us] = (h1[us, pl.ds(pl.multiple_of(sm * 16, 16), 16)].astype(F32) + r2[0, us].astype(F32) + r2[1, us].astype(F32) + r2[2, us].astype(F32)).astype(BF16)

    def rows16(yf):
        (fm, fd), (sm, sd) = axes(yf)
        return pl.ds(pl.multiple_of(fm * 64 + sm * 16, 16), 16)

    def rows64(yf):
        (fm, fd), (sm, sd) = axes(yf)
        return pl.ds(pl.multiple_of(fm * 64, 64), 64)

    def run(d):
        return dev(x, y, core, zh * 4 + mod4(zl + d))

    def za0():
        out_c = []
        for d in range(1, 4):
            p = mod4(zl + d)
            out_c.append(push(h2.at[pl.ds(p * 2, 2)], ra.at[d - 1], zas.at[0, d - 1], zar.at[0, d - 1], run(d)))
        return out_c

    def za1():
        rl[zl] = h2[8:12]
        return [push(h2.at[8:12], rl.at[zl], zas.at[1, d - 1], zar.at[1, d - 1], run(d)) for d in range(1, 4)]

    def far(src, dst, zi):
        return [push(src, dst, zbs.at[zi, d - 1], zbr.at[zi, d - 1], dev(x, y, core, lax.rem(z + 4 * d, 16))) for d in (2, 1, 3)]

    def sum4(ref):
        return ref[0].astype(F32) + ref[1].astype(F32) + ref[2].astype(F32) + ref[3].astype(F32)

    def zb0(c):
        for k in c:
            k.wait_recv()
        hz[0:2] = (h2[pl.ds(zl * 2, 2)].astype(F32) + ra[0].astype(F32) + ra[1].astype(F32) + ra[2].astype(F32)).astype(BF16)
        rb0[zh] = hz[0:2]
        pl.semaphore_wait(ready, 1)
        return far(hz.at[0:2], rb0.at[zh], 0)

    def zb1(c):
        for k in c:
            k.wait_recv()
        hz[2:6] = sum4(rl).astype(BF16)
        rb1[zh] = hz[2:6]
        return far(hz.at[2:6], rb1.at[zh], 1)

    def zc0(c):
        for k in c:
            k.wait_recv()
        flag = lax.div(zl, 2)
        r16 = pl.ds(pl.multiple_of((1 - flag) * (y * 64 + x * 16) + flag * (x * 64 + y * 16), 16), 16)
        us = pl.ds(zl * 2, 2)
        out[us, r16, mine] = sum4(rb0).astype(BF16)
        return [push(out.at[us, r16, mine], out.at[us, r16, mine], zcs.at[d - 1], zcr.at[d - 1], run(d)) for d in range(1, 4)]

    def zc1(c):
        for k in c:
            k.wait_recv()
        total = sum4(rb1).astype(BF16)
        out[8:10, rows16(True), mine] = total[0:2]
        out[10:12, rows16(False), mine] = total[2:4]

    def st5(ci):
        u0, n, yf = CHUNKS[ci]
        us = pl.ds(u0, n)
        r16 = rows16(yf)
        (fm, fd), (sm, sd) = axes(yf)
        return [push(out.at[us, r16, mine], out.at[us, r16, mine], g2s.at[ci, d - 1], g2r.at[ci, d - 1], sd(mod4(sm + d))) for d in range(1, 4)]

    def st6(ci, c):
        u0, n, yf = CHUNKS[ci]
        us = pl.ds(u0, n)
        for k in c:
            k.wait_recv()
        r64 = rows64(yf)
        (fm, fd), (sm, sd) = axes(yf)
        return [push(out.at[us, r64, mine], out.at[us, r64, mine], g1s.at[ci, d - 1], g1r.at[ci, d - 1], fd(mod4(fm + d))) for d in range(1, 4)]

    def st7(ci, c):
        u0, n, yf = CHUNKS[ci]
        us = pl.ds(u0, n)
        for k in c:
            k.wait_recv()
        return [push(out.at[us, :, mine], out.at[us, :, mine], g0s.at[ci], g0r.at[ci], sib)]


    state = [st0(0), st0(1), None, None]

    @pl.loop(0, 9)
    def _(t):
        rs = pl.ds(t * 2, 2)
        for b in range(3):
            s3[rs, :, b * 256 : b * 256 + 256] = sf[rs, 17 - b : 49 - b, :].astype(BF16)

    @pl.loop(0, 2)
    def _(t):
        acc = jnp.zeros((256, 256), F32)
        for a in range(3):
            for b in range(3):
                piece = s3[pl.ds(t * 8 + 2 - a, 8), :, b * 256 : b * 256 + 256].reshape(256, 256)
                acc += dot(piece, k2[a, b], ((1,), (1,)))
        ms[pl.ds(pl.multiple_of(t * 256, 256), 256)] = acc.astype(BF16)

    state[0] = st1(0, state[0])
    state[1] = st1(1, state[1])

    pack[11, 128:256, :] = dot(pool[2:18].reshape(512, 128), ms[...], ((0,), (0,))).astype(BF16)
    pack[11, 0:128, 128:256] = jnp.zeros((128, 128), BF16)

    @pl.loop(0, 4)
    def _(t):
        part = ms[pl.ds(pl.multiple_of(t * 128, 128), 128)]
        back = dot(part, proj[...], ((1,), (1,))).astype(BF16).astype(F32) * 0.25
        back = back.reshape(4, 32, 128)
        back = jnp.concatenate([back, back], axis=2)
        slope = d1[pl.ds(t * 8 + 4, 8)].reshape(4, 2, 32, 256)
        slope = jnp.stack([slope[:, 0] * back, slope[:, 1] * back], axis=1)
        s1[pl.ds(t * 8, 8)] = slope.reshape(8, 32, 256).astype(BF16)

    for a in range(3):
        grad = dot(xs[a + 4 : a + 36, 0:32].reshape(1024, 512), s1[...].reshape(1024, 256), ((0,), (0,)))
        for b in range(3):
            t = 3 * a + b
            tap = grad[b * 128 : b * 128 + 128, 0:128] + grad[b * 128 + 128 : b * 128 + 256, 128:256]
            pack[
                9 + t // 4, (t // 2) % 2 * 128 : (t // 2) % 2 * 128 + 128, t % 2 * 128 : t % 2 * 128 + 128
            ] = tap.astype(BF16)

    state[2], state[3] = st0(2), st0(3)
    state[0] = st2(0, state[0])
    state[1] = st2(1, state[1])
    state[2] = st1(2, state[2])
    state[3] = st1(3, state[3])
    st3(0, state[0])
    st3(1, state[1])
    first = za0()
    state[2] = st2(2, state[2])
    state[3] = st2(3, state[3])
    first = zb0(first)
    st3(2, state[2])
    st3(3, state[3])
    second = za1()
    second = zb1(second)
    first = zc0(first)
    for c in first:
        c.wait_recv()
    state[0], state[1] = st5(0), st5(1)
    zc1(second)
    state[2], state[3] = st5(2), st5(3)
    state[0], state[1] = st6(0, state[0]), st6(1, state[1])
    state[2], state[3] = st6(2, state[2]), st6(3, state[3])
    state[0], state[1] = st7(0, state[0]), st7(1, state[1])
    state[2], state[3] = st7(2, state[2]), st7(3, state[3])
    for c in state:
        for e in c:
            e.wait_recv()
    feat_copy.wait_recv()
    for c in sends:
        c.wait_send()


def network_call(img, k1, proj, k2, cot):
    V, D = pltpu.VMEM, pltpu.SemaphoreType.DMA
    n = len(CHUNKS)
    macs = 2 * 1000 * 1000 * 1000
    return pl.pallas_call(
        network,
        out_shape=(
            jax.ShapeDtypeStruct((UNITS, 256, 256), BF16),
            jax.ShapeDtypeStruct((16, 32, 256), BF16),
        ),
        in_specs=[pl.BlockSpec(memory_space=pltpu.HBM)] * 5,
        out_specs=(pl.BlockSpec(memory_space=pltpu.VMEM),) * 2,
        scratch_shapes=[
            V((32, 64, 128), BF16), V((3, 3, 128, 128), BF16), V((128, 256), BF16),
            V((3, 3, 256, 256), BF16), V((16, 32, 256), BF16), D((5,)),
            V((42, 112, 128), F32), V((42, 48, 512), BF16), V((3, 512, 256), BF16),
            V((40, 32, 256), F32), V((20, 32, 128), BF16), V((20, 64, 256), F32),
            V((20, 48, 768), BF16), V((18, 48, 256), F32), V((18, 64, 256), F32),
            V((18, 32, 256), BF16), V((18, 32, 768), BF16), V((512, 256), BF16),
            V((32, 32, 256), BF16), V((18, 32, 256), BF16), V((UNITS, 256, 256), BF16),
            V((2, 256, 128), BF16), V((2, 5, 64, 128), BF16), V((2, 256, 128), BF16),
            V((4, 48, 128), BF16), V((2, 16, 256), BF16), V((16, 32, 256), BF16),
            V((2, 32, 256), BF16), V((2, 3, 16, 256), BF16),
            V((UNITS, 256, 128), BF16), V((UNITS, 256, 128), BF16),
            V((3, UNITS, 64, 128), BF16), V((UNITS, 64, 128), BF16),
            V((3, UNITS, 16, 128), BF16), V((UNITS, 16, 128), BF16),
            V((3, 2, 16, 128), BF16), V((6, 16, 128), BF16), V((4, 2, 16, 128), BF16),
            V((4, 4, 16, 128), BF16), V((4, 4, 16, 128), BF16),
            D((8,)), D((8,)), D((9,)), D((9,)), D(()), D(()),
            D((n,)), D((n,)), D((n, 3)), D((n, 3)), D((n, 3)), D((n, 3)),
            D((2, 3)), D((2, 3)), D((2, 3)), D((2, 3)), D((3,)), D((3,)),
            D((n, 3)), D((n, 3)), D((n, 3)), D((n, 3)), D((n,)), D((n,)),
            pltpu.SemaphoreType.REGULAR,
        ],
        compiler_params=pltpu.CompilerParams(
            collective_id=0, has_side_effects=True, vmem_limit_bytes=56 << 20
        ),
        cost_estimate=pl.CostEstimate(
            flops=2 * macs, bytes_accessed=8 << 20, transcendentals=1 << 20
        ),
    )(img, k1, proj, k2, cot)


def widen(total, near, features, grad_first, grad_projection, grad_second):
    features[0] = near[...]
    for t in range(9):
        a, b = t // 3, t % 3
        row, lane = (t // 2) % 2 * 128, t % 2 * 128
        grad_second[a, b] = total[t].astype(F32)
        grad_first[a, b] = total[9 + t // 4, row : row + 128, lane : lane + 128].astype(F32)
    grad_projection[...] = total[11, 128:256, :].astype(F32)


def per_device(images, first_kernel, projection, second_kernel, cotangent):
    total, features = network_call(images[0], first_kernel, projection, second_kernel, cotangent[0])
    features, grad_first, grad_projection, grad_second = pl.pallas_call(
        widen,
        out_shape=(
            jax.ShapeDtypeStruct((1, 16, 32, 256), BF16),
            jax.ShapeDtypeStruct((3, 3, 128, 128), F32),
            jax.ShapeDtypeStruct((128, 256), F32),
            jax.ShapeDtypeStruct((3, 3, 256, 256), F32),
        ),
        in_specs=[pl.BlockSpec(memory_space=pltpu.VMEM)] * 2,
        out_specs=(pl.BlockSpec(memory_space=pltpu.VMEM),) * 4,
        compiler_params=pltpu.CompilerParams(vmem_limit_bytes=24 << 20),
    )(total, features)
    return (features, grad_first, grad_projection, grad_second)


def solution(mesh):
    placed = (P("section", "gy", "gx", None), P(), P(), P(), P("section", "gy", "gx", None))
    return jax.shard_map(
        per_device,
        mesh=mesh,
        in_specs=placed,
        out_specs=(P("section", "gy", "gx", None), P(), P(), P()),
        check_vma=False,
    )
```

```python
import functools

import jax
import jax.numpy as jnp
from jax import lax
from jax.experimental import pallas as pl
from jax.experimental.pallas import tpu as pltpu
from jax.sharding import PartitionSpec as P

MESH = pl.DeviceIdType.MESH
F32, BF16 = jnp.float32, jnp.bfloat16
UNITS = 12
CHUNKS = ((0, 4, True), (4, 4, False), (8, 2, True), (10, 2, False))
AROUND = ((-1, 0), (1, 0), (0, -1), (0, 1), (-1, -1), (-1, 1), (1, -1), (1, 1))


def coords():
    s, g, z = lax.axis_index("section"), lax.axis_index("gy"), lax.axis_index("gx")
    core = lax.rem(g, 2)
    x = s * 2 + lax.rem(lax.div(g, 2), 2)
    return x, lax.div(g, 4), core, z


def dev(x, y, core, z):
    return (lax.div(x, 2), y * 4 + lax.rem(x, 2) * 2 + core, z)


def mod4(v):
    return lax.rem(v, 4)


def dot(left, right, dims=((1,), (0,))):
    return lax.dot_general(left, right, (dims, ((), ())), preferred_element_type=F32)


def sigmoid(v):
    return 0.5 * jnp.tanh(0.5 * v) + 0.5


def network(
    img_in, k1_in, proj_in, k2_in, cot_h, out_h, feat,
    out, leave,
    img, k1, proj, k2, cot, fetch,
    xf, xs, w1, d1, pool, mf, m3, cotf, slopes, sf, si, s3, ms, s1, fb, pack,
    colpack, rows_in, cols_in, corners_in, cotpack, cot_in, cot_rows, cot_cols,
    r0, h0, r1, h1, r2, h2, ra, hz, rb0, rl, rb1,
    hs, hr, cs, cr, fs, fr,
    s0s, s0r, s1s, s1r, s2s, s2r, zas, zar, zbs, zbr, zcs, zcr, g2s, g2r, g1s, g1r, g0s, g0r, ready,
):
    x, y, core, z = coords()
    sec, gy = lax.axis_index("section"), lax.axis_index("gy")
    other_sec = 1 - sec
    sib = dev(x, y, 1 - core, z)

    def near(s, dy, dx):
        return (s, lax.rem(gy + dy + 16, 16), lax.rem(z + dx + 16, 16))

    barrier = pltpu.get_barrier_semaphore()

    def greet(to):
        pl.semaphore_signal(barrier, inc=1, device_id=to, device_id_type=MESH)

    for dy, dx in AROUND:
        greet(near(sec, dy, dx))
        greet(near(other_sec, dy, dx))
    greet(near(other_sec, 0, 0))
    greet(sib)
    for d in range(1, 4):
        greet(dev(mod4(x + d), y, core, z))
        greet(dev(x, mod4(y + d), core, z))
    zl, zh = mod4(z), lax.div(z, 4)
    for d in range(1, 4):
        greet(dev(x, y, core, zh * 4 + mod4(zl + d)))
    greet(dev(x, y, core, lax.rem(z + 4, 16)))
    greet(dev(x, y, core, lax.rem(z + 12, 16)))

    fetches = [
        pltpu.make_async_copy(src, dst, fetch.at[i])
        for i, (src, dst) in enumerate(
            ((img_in, img), (cot_h, cot), (k1_in, k1), (proj_in, proj), (k2_in, k2))
        )
    ]
    for c in fetches:
        c.start()
    fetches[0].wait()
    xf[5:37, 24:88] = img[...].astype(F32)
    colpack[0] = xf[5:37, 24:32].reshape(256, 128).astype(BF16)
    colpack[1] = xf[5:37, 80:88].reshape(256, 128).astype(BF16)
    fetches[1].wait()
    cotf[0:16, 0:32] = cot[...].astype(F32)
    cotpack[0] = cotf[0:16, 0, :].astype(BF16)
    cotpack[1] = cotf[0:16, 31, :].astype(BF16)

    pl.semaphore_wait(barrier, 29)
    pl.semaphore_signal(
        ready, inc=1, device_id=dev(x, y, core, lax.rem(z + 12, 16)), device_id_type=MESH
    )
    sends = []

    def push(src, dst, ss, rs, to):
        c = pltpu.make_async_remote_copy(
            src_ref=src, dst_ref=dst, send_sem=ss, recv_sem=rs, device_id=to, device_id_type=MESH
        )
        c.start()
        sends.append(c)
        return c

    halo = [
        push(img.at[0:5], rows_in.at[1], hs.at[0], hr.at[0], near(sec, -1, 0)),
        push(img.at[27:32], rows_in.at[0], hs.at[1], hr.at[1], near(sec, 1, 0)),
        push(colpack.at[0], cols_in.at[1], hs.at[2], hr.at[2], near(sec, 0, -1)),
        push(colpack.at[1], cols_in.at[0], hs.at[3], hr.at[3], near(sec, 0, 1)),
        push(colpack.at[0, 0:48], corners_in.at[3], hs.at[4], hr.at[4], near(sec, -1, -1)),
        push(colpack.at[1, 0:48], corners_in.at[2], hs.at[5], hr.at[5], near(sec, -1, 1)),
        push(colpack.at[0, 208:256], corners_in.at[1], hs.at[6], hr.at[6], near(sec, 1, -1)),
        push(colpack.at[1, 208:256], corners_in.at[0], hs.at[7], hr.at[7], near(sec, 1, 1)),
    ]
    cots = [
        push(cot, cot_in, cs.at[0], cr.at[0], near(other_sec, 0, 0)),
        push(cot.at[0], cot_rows.at[1], cs.at[1], cr.at[1], near(other_sec, -1, 0)),
        push(cot.at[15], cot_rows.at[0], cs.at[2], cr.at[2], near(other_sec, 1, 0)),
        push(cotpack.at[0], cot_cols.at[1, 1], cs.at[3], cr.at[3], near(other_sec, 0, -1)),
        push(cotpack.at[1], cot_cols.at[0, 1], cs.at[4], cr.at[4], near(other_sec, 0, 1)),
        push(cotpack.at[0], cot_cols.at[1, 2], cs.at[5], cr.at[5], near(other_sec, -1, -1)),
        push(cotpack.at[1], cot_cols.at[0, 2], cs.at[6], cr.at[6], near(other_sec, -1, 1)),
        push(cotpack.at[0], cot_cols.at[1, 0], cs.at[7], cr.at[7], near(other_sec, 1, -1)),
        push(cotpack.at[1], cot_cols.at[0, 0], cs.at[8], cr.at[8], near(other_sec, 1, 1)),
    ]

    fetches[2].wait()
    zero = jnp.zeros((128, 128), BF16)
    for a in range(3):
        w1[a, 384:512, 0:128] = zero
        w1[a, 0:128, 128:256] = zero
        for b in range(3):
            w1[a, b * 128 : b * 128 + 128, 0:128] = k1[a, b]
            w1[a, b * 128 + 128 : b * 128 + 256, 128:256] = k1[a, b]
    xf[:, 0:16] = jnp.zeros((42, 16, 128), F32)
    xf[:, 96:112] = jnp.zeros((42, 16, 128), F32)
    mf[:, 0:8] = jnp.zeros((20, 8, 256), F32)
    mf[:, 56:64] = jnp.zeros((20, 8, 256), F32)
    cotf[...] = jnp.zeros((18, 48, 256), F32)

    fetches[3].wait()
    fetches[4].wait()
    for c in halo:
        c.wait_recv()
    xf[0:5, 24:88] = rows_in[0].astype(F32)
    xf[37:42, 24:88] = rows_in[1].astype(F32)
    for side, at in ((0, 16), (1, 88)):
        xf[5:37, at : at + 8] = cols_in[side].astype(F32).reshape(32, 8, 128)
        xf[0:5, at : at + 8] = corners_in[side].astype(F32).reshape(6, 8, 128)[1:6]
        xf[37:42, at : at + 8] = corners_in[2 + side].astype(F32).reshape(6, 8, 128)[0:5]

    @pl.when(gy == 0)
    def _():
        xf[0:5, 16:96] = jnp.zeros((5, 80, 128), F32)

    @pl.when(gy == 15)
    def _():
        xf[37:42, 16:96] = jnp.zeros((5, 80, 128), F32)

    @pl.when(z == 0)
    def _():
        xf[:, 16:24] = jnp.zeros((42, 8, 128), F32)

    @pl.when(z == 15)
    def _():
        xf[:, 88:96] = jnp.zeros((42, 8, 128), F32)

    @pl.loop(0, 21)
    def _(t):
        rs = pl.ds(t * 2, 2)
        for p in range(4):
            lanes = slice(p * 128, p * 128 + 128)
            xs[rs, 0:32, lanes] = xf[rs, pl.ds(23 + p, 32, 2), :].astype(BF16)
            right = xf[rs, pl.ds(87 + p, 8, 2), :]
            left = xf[rs, pl.ds(7 + p, 8, 2), :]
            xs[rs, 32:48, lanes] = jnp.concatenate([right, left], axis=1).astype(BF16)

    @pl.loop(0, 5)
    def _(t):
        acc = dot(xs[pl.ds(t * 8, 8)].reshape(384, 512), w1[0])
        acc += dot(xs[pl.ds(t * 8 + 1, 8)].reshape(384, 512), w1[1])
        acc += dot(xs[pl.ds(t * 8 + 2, 8)].reshape(384, 512), w1[2])
        sig = sigmoid(acc)
        hid = (acc * sig).astype(BF16).astype(F32).reshape(4, 2, 48, 256)
        slope = sig * (1.0 + acc * (1.0 - sig))
        d1[pl.ds(t * 8, 8)] = slope.reshape(8, 48, 256)[:, 0:32]
        total = hid[:, 0] + hid[:, 1]
        total = (total[:, :, 0:128] + total[:, :, 128:256]) * 0.25
        row = lax.broadcasted_iota(jnp.int32, (4, 48, 128), 0) + (t * 4 - 2 + gy * 16)
        k = lax.broadcasted_iota(jnp.int32, (4, 48, 128), 1)
        col = jnp.where(k < 40, k, k - 48) + z * 32
        inside = (row >= 0) & (row < 256) & (col >= 0) & (col < 512)
        pooled = jnp.where(inside, total, 0.0).astype(BF16)
        pool[pl.ds(t * 4, 4)] = pooled[:, 0:32]
        mid = dot(pooled.reshape(192, 128), proj[...]).astype(BF16).astype(F32).reshape(4, 48, 256)
        mf[pl.ds(t * 4, 4), 16:56] = mid[:, 0:40]
        mf[pl.ds(t * 4, 4), 8:16] = mid[:, 40:48]

    @pl.loop(0, 10)
    def _(t):
        rs = pl.ds(t * 2, 2)
        for b in range(3):
            lanes = slice(b * 256, b * 256 + 256)
            m3[rs, 0:32, lanes] = mf[rs, 15 + b : 47 + b, :].astype(BF16)
            sides = [mf[rs, 47 + b : 55 + b, :], mf[rs, 7 + b : 15 + b, :]]
            m3[rs, 32:48, lanes] = jnp.concatenate(sides, axis=1).astype(BF16)

    @pl.loop(0, 3)
    def _(t):
        acc = dot(m3[pl.ds(t * 6, 6)].reshape(288, 768), k2[0].reshape(768, 256))
        acc += dot(m3[pl.ds(t * 6 + 1, 6)].reshape(288, 768), k2[1].reshape(768, 256))
        acc += dot(m3[pl.ds(t * 6 + 2, 6)].reshape(288, 768), k2[2].reshape(768, 256))
        sig = sigmoid(acc)
        fb[pl.ds(t * 6, 6)] = (acc * sig).astype(BF16).reshape(6, 48, 256)[:, 0:32]
        slopes[pl.ds(t * 6, 6)] = (sig * (1.0 + acc * (1.0 - sig))).reshape(6, 48, 256)

    feat_copy = push(fb.at[1:17], feat, fs, fr, near(other_sec, 0, 0))

    for c in cots:
        c.wait_recv()
    cotf[1:17, 0:32] = cot_in[...].astype(F32)
    cotf[0, 0:32] = cot_rows[0].astype(F32)
    cotf[17, 0:32] = cot_rows[1].astype(F32)
    for side, at in ((0, 47), (1, 32)):
        column = cot_cols[side, 1].astype(F32)
        for q in range(16):
            cotf[1 + q, at : at + 1, :] = column[q : q + 1]
        cotf[0, at : at + 1, :] = cot_cols[side, 0].astype(F32)[15:16]
        cotf[17, at : at + 1, :] = cot_cols[side, 2].astype(F32)[0:1]

    @pl.when(gy == 0)
    def _():
        cotf[0] = jnp.zeros((48, 256), F32)

    @pl.when(gy == 15)
    def _():
        cotf[17] = jnp.zeros((48, 256), F32)

    @pl.when(z == 0)
    def _():
        cotf[:, 40:48] = jnp.zeros((18, 8, 256), F32)

    @pl.when(z == 15)
    def _():
        cotf[:, 32:40] = jnp.zeros((18, 8, 256), F32)

    @pl.loop(0, 3)
    def _(t):
        slope = (slopes[pl.ds(t * 6, 6)] * cotf[pl.ds(t * 6, 6)]).astype(BF16)
        si[pl.ds(t * 6, 6)] = slope[:, 0:32]
        slope = slope.astype(F32)
        sf[pl.ds(t * 6, 6), 16:56] = slope[:, 0:40]
        sf[pl.ds(t * 6, 6), 8:16] = slope[:, 40:48]


    for a in range(3):
        grad = dot(m3[a + 1 : a + 17, 0:32].reshape(512, 768), si[1:17].reshape(512, 256), ((0,), (0,)))
        pack[3 * a : 3 * a + 3] = grad.reshape(3, 256, 256).astype(BF16)

    mine = pl.ds(pl.multiple_of(core * 128, 128), 128)
    other = pl.ds(pl.multiple_of((1 - core) * 128, 128), 128)

    def axes(yfirst):
        if yfirst:
            return (y, lambda p: dev(x, p, core, z)), (x, lambda p: dev(p, y, core, z))
        return (x, lambda p: dev(p, y, core, z)), (y, lambda p: dev(x, p, core, z))

    def st0(ci):
        u0, n, yf = CHUNKS[ci]
        us = pl.ds(u0, n)
        return [push(pack.at[us, :, other], r0.at[us], s0s.at[ci], s0r.at[ci], sib)]

    def st1(ci, c):
        u0, n, yf = CHUNKS[ci]
        us = pl.ds(u0, n)
        c[0].wait_recv()
        h0[us] = (pack[us, :, mine].astype(F32) + r0[us].astype(F32)).astype(BF16)
        (fm, fd), _ = axes(yf)
        out_c = []
        for d in range(1, 4):
            p = mod4(fm + d)
            out_c.append(push(h0.at[us, pl.ds(pl.multiple_of(p * 64, 64), 64)], r1.at[d - 1, us], s1s.at[ci, d - 1], s1r.at[ci, d - 1], fd(p)))
        return out_c

    def st2(ci, c):
        u0, n, yf = CHUNKS[ci]
        us = pl.ds(u0, n)
        for k in c:
            k.wait_recv()
        (fm, fd), (sm, sd) = axes(yf)
        h1[us] = (h0[us, pl.ds(pl.multiple_of(fm * 64, 64), 64)].astype(F32) + r1[0, us].astype(F32) + r1[1, us].astype(F32) + r1[2, us].astype(F32)).astype(BF16)
        out_c = []
        for d in range(1, 4):
            p = mod4(sm + d)
            out_c.append(push(h1.at[us, pl.ds(pl.multiple_of(p * 16, 16), 16)], r2.at[d - 1, us], s2s.at[ci, d - 1], s2r.at[ci, d - 1], sd(p)))
        return out_c

    def st3(ci, c):
        u0, n, yf = CHUNKS[ci]
        us = pl.ds(u0, n)
        for k in c:
            k.wait_recv()
        (fm, fd), (sm, sd) = axes(yf)
        h2[us] = (h1[us, pl.ds(pl.multiple_of(sm * 16, 16), 16)].astype(F32) + r2[0, us].astype(F32) + r2[1, us].astype(F32) + r2[2, us].astype(F32)).astype(BF16)

    def rows16(yf):
        (fm, fd), (sm, sd) = axes(yf)
        return pl.ds(pl.multiple_of(fm * 64 + sm * 16, 16), 16)

    def rows64(yf):
        (fm, fd), (sm, sd) = axes(yf)
        return pl.ds(pl.multiple_of(fm * 64, 64), 64)

    def run(d):
        return dev(x, y, core, zh * 4 + mod4(zl + d))

    def za0():
        out_c = []
        for d in range(1, 4):
            p = mod4(zl + d)
            out_c.append(push(h2.at[pl.ds(p * 2, 2)], ra.at[d - 1], zas.at[0, d - 1], zar.at[0, d - 1], run(d)))
        return out_c

    def za1():
        rl[zl] = h2[8:12]
        return [push(h2.at[8:12], rl.at[zl], zas.at[1, d - 1], zar.at[1, d - 1], run(d)) for d in range(1, 4)]

    def far(src, dst, zi):
        return [push(src, dst, zbs.at[zi, d - 1], zbr.at[zi, d - 1], dev(x, y, core, lax.rem(z + 4 * d, 16))) for d in (2, 1, 3)]

    def sum4(ref):
        return ref[0].astype(F32) + ref[1].astype(F32) + ref[2].astype(F32) + ref[3].astype(F32)

    def zb0(c):
        for k in c:
            k.wait_recv()
        hz[0:2] = (h2[pl.ds(zl * 2, 2)].astype(F32) + ra[0].astype(F32) + ra[1].astype(F32) + ra[2].astype(F32)).astype(BF16)
        rb0[zh] = hz[0:2]
        pl.semaphore_wait(ready, 1)
        return far(hz.at[0:2], rb0.at[zh], 0)

    def zb1(c):
        for k in c:
            k.wait_recv()
        hz[2:6] = sum4(rl).astype(BF16)
        rb1[zh] = hz[2:6]
        return far(hz.at[2:6], rb1.at[zh], 1)

    def zc0(c):
        for k in c:
            k.wait_recv()
        flag = lax.div(zl, 2)
        r16 = pl.ds(pl.multiple_of((1 - flag) * (y * 64 + x * 16) + flag * (x * 64 + y * 16), 16), 16)
        us = pl.ds(zl * 2, 2)
        out[us, r16, mine] = sum4(rb0).astype(BF16)
        return [push(out.at[us, r16, mine], out.at[us, r16, mine], zcs.at[d - 1], zcr.at[d - 1], run(d)) for d in range(1, 4)]

    def zc1(c):
        for k in c:
            k.wait_recv()
        total = sum4(rb1).astype(BF16)
        out[8:10, rows16(True), mine] = total[0:2]
        out[10:12, rows16(False), mine] = total[2:4]

    def st5(ci):
        u0, n, yf = CHUNKS[ci]
        us = pl.ds(u0, n)
        r16 = rows16(yf)
        (fm, fd), (sm, sd) = axes(yf)
        return [push(out.at[us, r16, mine], out.at[us, r16, mine], g2s.at[ci, d - 1], g2r.at[ci, d - 1], sd(mod4(sm + d))) for d in range(1, 4)]

    def st6(ci, c):
        u0, n, yf = CHUNKS[ci]
        us = pl.ds(u0, n)
        for k in c:
            k.wait_recv()
        r64 = rows64(yf)
        (fm, fd), (sm, sd) = axes(yf)
        return [push(out.at[us, r64, mine], out.at[us, r64, mine], g1s.at[ci, d - 1], g1r.at[ci, d - 1], fd(mod4(fm + d))) for d in range(1, 4)]

    def st7(ci, c):
        u0, n, yf = CHUNKS[ci]
        us = pl.ds(u0, n)
        for k in c:
            k.wait_recv()
        return [push(out.at[us, :, mine], out.at[us, :, mine], g0s.at[ci], g0r.at[ci], sib)]


    state = [st0(0), st0(1), None, None]

    @pl.loop(0, 9)
    def _(t):
        rs = pl.ds(t * 2, 2)
        for b in range(3):
            s3[rs, :, b * 256 : b * 256 + 256] = sf[rs, 17 - b : 49 - b, :].astype(BF16)

    @pl.loop(0, 2)
    def _(t):
        acc = jnp.zeros((256, 256), F32)
        for a in range(3):
            for b in range(3):
                piece = s3[pl.ds(t * 8 + 2 - a, 8), :, b * 256 : b * 256 + 256].reshape(256, 256)
                acc += dot(piece, k2[a, b], ((1,), (1,)))
        ms[pl.ds(pl.multiple_of(t * 256, 256), 256)] = acc.astype(BF16)

    state[0] = st1(0, state[0])
    state[1] = st1(1, state[1])

    pack[11, 128:256, :] = dot(pool[2:18].reshape(512, 128), ms[...], ((0,), (0,))).astype(BF16)
    pack[11, 0:128, 128:256] = jnp.zeros((128, 128), BF16)

    @pl.loop(0, 4)
    def _(t):
        part = ms[pl.ds(pl.multiple_of(t * 128, 128), 128)]
        back = dot(part, proj[...], ((1,), (1,))).astype(BF16).astype(F32) * 0.25
        back = back.reshape(4, 32, 128)
        back = jnp.concatenate([back, back], axis=2)
        slope = d1[pl.ds(t * 8 + 4, 8)].reshape(4, 2, 32, 256)
        slope = jnp.stack([slope[:, 0] * back, slope[:, 1] * back], axis=1)
        s1[pl.ds(t * 8, 8)] = slope.reshape(8, 32, 256).astype(BF16)

    for a in range(3):
        grad = dot(xs[a + 4 : a + 36, 0:32].reshape(1024, 512), s1[...].reshape(1024, 256), ((0,), (0,)))
        for b in range(3):
            t = 3 * a + b
            tap = grad[b * 128 : b * 128 + 128, 0:128] + grad[b * 128 + 128 : b * 128 + 256, 128:256]
            pack[
                9 + t // 4, (t // 2) % 2 * 128 : (t // 2) % 2 * 128 + 128, t % 2 * 128 : t % 2 * 128 + 128
            ] = tap.astype(BF16)

    state[2], state[3] = st0(2), st0(3)
    state[0] = st2(0, state[0])
    state[1] = st2(1, state[1])
    state[2] = st1(2, state[2])
    state[3] = st1(3, state[3])
    st3(0, state[0])
    st3(1, state[1])
    first = za0()
    state[2] = st2(2, state[2])
    state[3] = st2(3, state[3])
    first = zb0(first)
    st3(2, state[2])
    st3(3, state[3])
    second = za1()
    second = zb1(second)
    first = zc0(first)
    for c in first:
        c.wait_recv()
    state[0], state[1] = st5(0), st5(1)
    zc1(second)
    state[2], state[3] = st5(2), st5(3)
    state[0], state[1] = st6(0, state[0]), st6(1, state[1])
    state[2], state[3] = st6(2, state[2]), st6(3, state[3])
    state[0], state[1] = st7(0, state[0]), st7(1, state[1])
    state[2], state[3] = st7(2, state[2]), st7(3, state[3])
    leaves = []
    for half, (u, n) in enumerate(((0, 8), (8, 4))):
        for c in state[2 * half : 2 * half + 2]:
            for e in c:
                e.wait_recv()
        c = pltpu.make_async_copy(out.at[u : u + n], out_h.at[u : u + n], leave.at[half])
        c.start()
        leaves.append(c)
    for c in leaves:
        c.wait()
    feat_copy.wait_recv()
    for c in sends:
        c.wait_send()


def network_call(img, k1, proj, k2, cot):
    V, D = pltpu.VMEM, pltpu.SemaphoreType.DMA
    n = len(CHUNKS)
    macs = 2 * 1000 * 1000 * 1000
    return pl.pallas_call(
        network,
        out_shape=(
            jax.ShapeDtypeStruct((UNITS, 256, 256), BF16),
            jax.ShapeDtypeStruct((16, 32, 256), BF16),
        ),
        in_specs=[pl.BlockSpec(memory_space=pltpu.HBM)] * 5,
        out_specs=(pl.BlockSpec(memory_space=pltpu.HBM),) * 2,
        scratch_shapes=[
            V((UNITS, 256, 256), BF16), D((2,)),
            V((32, 64, 128), BF16), V((3, 3, 128, 128), BF16), V((128, 256), BF16),
            V((3, 3, 256, 256), BF16), V((16, 32, 256), BF16), D((5,)),
            V((42, 112, 128), F32), V((42, 48, 512), BF16), V((3, 512, 256), BF16),
            V((40, 32, 256), F32), V((20, 32, 128), BF16), V((20, 64, 256), F32),
            V((20, 48, 768), BF16), V((18, 48, 256), F32), V((18, 48, 256), F32), V((18, 64, 256), F32),
            V((18, 32, 256), BF16), V((18, 32, 768), BF16), V((512, 256), BF16),
            V((32, 32, 256), BF16), V((18, 32, 256), BF16), V((UNITS, 256, 256), BF16),
            V((2, 256, 128), BF16), V((2, 5, 64, 128), BF16), V((2, 256, 128), BF16),
            V((4, 48, 128), BF16), V((2, 16, 256), BF16), V((16, 32, 256), BF16),
            V((2, 32, 256), BF16), V((2, 3, 16, 256), BF16),
            V((UNITS, 256, 128), BF16), V((UNITS, 256, 128), BF16),
            V((3, UNITS, 64, 128), BF16), V((UNITS, 64, 128), BF16),
            V((3, UNITS, 16, 128), BF16), V((UNITS, 16, 128), BF16),
            V((3, 2, 16, 128), BF16), V((6, 16, 128), BF16), V((4, 2, 16, 128), BF16),
            V((4, 4, 16, 128), BF16), V((4, 4, 16, 128), BF16),
            D((8,)), D((8,)), D((9,)), D((9,)), D(()), D(()),
            D((n,)), D((n,)), D((n, 3)), D((n, 3)), D((n, 3)), D((n, 3)),
            D((2, 3)), D((2, 3)), D((2, 3)), D((2, 3)), D((3,)), D((3,)),
            D((n, 3)), D((n, 3)), D((n, 3)), D((n, 3)), D((n,)), D((n,)),
            pltpu.SemaphoreType.REGULAR,
        ],
        compiler_params=pltpu.CompilerParams(
            collective_id=0, has_side_effects=True, vmem_limit_bytes=56 << 20
        ),
        cost_estimate=pl.CostEstimate(
            flops=2 * macs, bytes_accessed=8 << 20, transcendentals=1 << 20
        ),
    )(img, k1, proj, k2, cot)


def widen(
    total, near, features, grad_first, grad_projection, grad_second,
    narrow, first, projection, second, feat, in_sems, out_sems,
):
    cuts = ((9, 3), (0, 3), (3, 3), (6, 3))
    loads = [
        pltpu.make_async_copy(total.at[u : u + n], narrow.at[u : u + n], in_sems.at[i])
        for i, (u, n) in enumerate(cuts)
    ] + [pltpu.make_async_copy(near, feat, in_sems.at[4])]
    for c in loads:
        c.start()
    stores = []

    def store(src, dst):
        c = pltpu.make_async_copy(src, dst, out_sems.at[len(stores)])
        c.start()
        stores.append(c)

    loads[0].wait()
    for t in range(9):
        row, lane = (t // 2) % 2 * 128, t % 2 * 128
        first[t // 3, t % 3] = narrow[9 + t // 4, row : row + 128, lane : lane + 128].astype(F32)
    projection[...] = narrow[11, 128:256, :].astype(F32)
    store(first, grad_first)
    store(projection, grad_projection)
    for a in range(3):
        loads[1 + a].wait()
        for b in range(3):
            second[a, b] = narrow[3 * a + b].astype(F32)
        store(second.at[a], grad_second.at[a])
    loads[4].wait()
    store(feat, features.at[0])
    for c in stores:
        c.wait()


def per_device(images, first_kernel, projection, second_kernel, cotangent):
    total, features = network_call(images[0], first_kernel, projection, second_kernel, cotangent[0])
    features, grad_first, grad_projection, grad_second = pl.pallas_call(
        widen,
        out_shape=(
            jax.ShapeDtypeStruct((1, 16, 32, 256), BF16),
            jax.ShapeDtypeStruct((3, 3, 128, 128), F32),
            jax.ShapeDtypeStruct((128, 256), F32),
            jax.ShapeDtypeStruct((3, 3, 256, 256), F32),
        ),
        in_specs=[pl.BlockSpec(memory_space=pltpu.HBM)] * 2,
        out_specs=(pl.BlockSpec(memory_space=pltpu.HBM),) * 4,
        scratch_shapes=[
            pltpu.VMEM((UNITS, 256, 256), BF16), pltpu.VMEM((3, 3, 128, 128), F32),
            pltpu.VMEM((128, 256), F32), pltpu.VMEM((3, 3, 256, 256), F32),
            pltpu.VMEM((16, 32, 256), BF16),
            pltpu.SemaphoreType.DMA((5,)), pltpu.SemaphoreType.DMA((6,)),
        ],
        compiler_params=pltpu.CompilerParams(vmem_limit_bytes=60 << 20),
    )(total, features)
    return (features, grad_first, grad_projection, grad_second)


def solution(mesh):
    placed = (P("section", "gy", "gx", None), P(), P(), P(), P("section", "gy", "gx", None))
    return jax.shard_map(
        per_device,
        mesh=mesh,
        in_specs=placed,
        out_specs=(P("section", "gy", "gx", None), P(), P(), P()),
        check_vma=False,
    )
```

```python
import functools

import jax
import jax.numpy as jnp
from jax import lax
from jax.experimental import pallas as pl
from jax.experimental.pallas import tpu as pltpu
from jax.sharding import PartitionSpec as P

MESH = pl.DeviceIdType.MESH
F32, BF16 = jnp.float32, jnp.bfloat16
UNITS = 12
CHUNKS = ((0, 4, True), (4, 4, False), (8, 2, True), (10, 2, False))
AROUND = ((-1, 0), (1, 0), (0, -1), (0, 1), (-1, -1), (-1, 1), (1, -1), (1, 1))


def coords():
    s, g, z = lax.axis_index("section"), lax.axis_index("gy"), lax.axis_index("gx")
    core = lax.rem(g, 2)
    x = s * 2 + lax.rem(lax.div(g, 2), 2)
    return x, lax.div(g, 4), core, z


def dev(x, y, core, z):
    return (lax.div(x, 2), y * 4 + lax.rem(x, 2) * 2 + core, z)


def mod4(v):
    return lax.rem(v, 4)


def dot(left, right, dims=((1,), (0,))):
    return lax.dot_general(left, right, (dims, ((), ())), preferred_element_type=F32)


def sigmoid(v):
    return 0.5 * jnp.tanh(0.5 * v) + 0.5


def network(
    img_in, k1_in, proj_in, k2_in, cot_h, out_h, feat,
    out, leave,
    img, k1, proj, k2, cot, fetch,
    xf, xs, w1, d1, pool, mf, m3, cotf, slopes, sf, si, s3, ms, s1, fb, pack,
    colpack, rows_in, cols_in, corners_in, cotpack, cot_in, cot_rows, cot_cols,
    r0, h0, r1, h1, r2, h2, ra, hz, rb0, rl, rb1,
    hs, hr, cs, cr, fs, fr,
    s0s, s0r, s1s, s1r, s2s, s2r, zas, zar, zbs, zbr, zcs, zcr, g2s, g2r, g1s, g1r, g0s, g0r, ready,
):
    x, y, core, z = coords()
    sec, gy = lax.axis_index("section"), lax.axis_index("gy")
    other_sec = 1 - sec
    sib = dev(x, y, 1 - core, z)

    def near(s, dy, dx):
        return (s, lax.rem(gy + dy + 16, 16), lax.rem(z + dx + 16, 16))

    barrier = pltpu.get_barrier_semaphore()

    def greet(to):
        pl.semaphore_signal(barrier, inc=1, device_id=to, device_id_type=MESH)

    for dy, dx in AROUND:
        greet(near(sec, dy, dx))
        greet(near(other_sec, dy, dx))
    greet(near(other_sec, 0, 0))
    greet(sib)
    for d in range(1, 4):
        greet(dev(mod4(x + d), y, core, z))
        greet(dev(x, mod4(y + d), core, z))
    zl, zh = mod4(z), lax.div(z, 4)
    for d in range(1, 4):
        greet(dev(x, y, core, zh * 4 + mod4(zl + d)))
    greet(dev(x, y, core, lax.rem(z + 4, 16)))
    greet(dev(x, y, core, lax.rem(z + 12, 16)))

    fetches = [
        pltpu.make_async_copy(src, dst, fetch.at[i])
        for i, (src, dst) in enumerate(
            ((img_in, img), (cot_h, cot), (k1_in, k1), (proj_in, proj), (k2_in, k2))
        )
    ]
    for c in fetches:
        c.start()
    fetches[0].wait()
    xf[5:37, 24:88] = img[...].astype(F32)
    colpack[0] = xf[5:37, 24:32].reshape(256, 128).astype(BF16)
    colpack[1] = xf[5:37, 80:88].reshape(256, 128).astype(BF16)
    fetches[1].wait()
    cotf[0:16, 0:32] = cot[...].astype(F32)
    cotpack[0] = cotf[0:16, 0, :].astype(BF16)
    cotpack[1] = cotf[0:16, 31, :].astype(BF16)

    pl.semaphore_wait(barrier, 29)
    pl.semaphore_signal(
        ready, inc=1, device_id=dev(x, y, core, lax.rem(z + 12, 16)), device_id_type=MESH
    )
    sends = []

    def push(src, dst, ss, rs, to):
        c = pltpu.make_async_remote_copy(
            src_ref=src, dst_ref=dst, send_sem=ss, recv_sem=rs, device_id=to, device_id_type=MESH
        )
        c.start()
        sends.append(c)
        return c

    halo = [
        push(img.at[0:5], rows_in.at[1], hs.at[0], hr.at[0], near(sec, -1, 0)),
        push(img.at[27:32], rows_in.at[0], hs.at[1], hr.at[1], near(sec, 1, 0)),
        push(colpack.at[0], cols_in.at[1], hs.at[2], hr.at[2], near(sec, 0, -1)),
        push(colpack.at[1], cols_in.at[0], hs.at[3], hr.at[3], near(sec, 0, 1)),
        push(colpack.at[0, 0:48], corners_in.at[3], hs.at[4], hr.at[4], near(sec, -1, -1)),
        push(colpack.at[1, 0:48], corners_in.at[2], hs.at[5], hr.at[5], near(sec, -1, 1)),
        push(colpack.at[0, 208:256], corners_in.at[1], hs.at[6], hr.at[6], near(sec, 1, -1)),
        push(colpack.at[1, 208:256], corners_in.at[0], hs.at[7], hr.at[7], near(sec, 1, 1)),
    ]
    cots = [
        push(cot, cot_in, cs.at[0], cr.at[0], near(other_sec, 0, 0)),
        push(cot.at[0], cot_rows.at[1], cs.at[1], cr.at[1], near(other_sec, -1, 0)),
        push(cot.at[15], cot_rows.at[0], cs.at[2], cr.at[2], near(other_sec, 1, 0)),
        push(cotpack.at[0], cot_cols.at[1, 1], cs.at[3], cr.at[3], near(other_sec, 0, -1)),
        push(cotpack.at[1], cot_cols.at[0, 1], cs.at[4], cr.at[4], near(other_sec, 0, 1)),
        push(cotpack.at[0], cot_cols.at[1, 2], cs.at[5], cr.at[5], near(other_sec, -1, -1)),
        push(cotpack.at[1], cot_cols.at[0, 2], cs.at[6], cr.at[6], near(other_sec, -1, 1)),
        push(cotpack.at[0], cot_cols.at[1, 0], cs.at[7], cr.at[7], near(other_sec, 1, -1)),
        push(cotpack.at[1], cot_cols.at[0, 0], cs.at[8], cr.at[8], near(other_sec, 1, 1)),
    ]

    fetches[2].wait()
    zero = jnp.zeros((128, 128), BF16)
    for a in range(3):
        w1[a, 384:512, 0:128] = zero
        w1[a, 0:128, 128:256] = zero
        for b in range(3):
            w1[a, b * 128 : b * 128 + 128, 0:128] = k1[a, b]
            w1[a, b * 128 + 128 : b * 128 + 256, 128:256] = k1[a, b]
    xf[:, 0:16] = jnp.zeros((42, 16, 128), F32)
    xf[:, 96:112] = jnp.zeros((42, 16, 128), F32)
    mf[:, 0:8] = jnp.zeros((20, 8, 256), F32)
    mf[:, 56:64] = jnp.zeros((20, 8, 256), F32)
    cotf[...] = jnp.zeros((18, 48, 256), F32)

    fetches[3].wait()
    fetches[4].wait()
    for c in halo:
        c.wait_recv()
    xf[0:5, 24:88] = rows_in[0].astype(F32)
    xf[37:42, 24:88] = rows_in[1].astype(F32)
    for side, at in ((0, 16), (1, 88)):
        xf[5:37, at : at + 8] = cols_in[side].astype(F32).reshape(32, 8, 128)
        xf[0:5, at : at + 8] = corners_in[side].astype(F32).reshape(6, 8, 128)[1:6]
        xf[37:42, at : at + 8] = corners_in[2 + side].astype(F32).reshape(6, 8, 128)[0:5]

    @pl.when(gy == 0)
    def _():
        xf[0:5, 16:96] = jnp.zeros((5, 80, 128), F32)

    @pl.when(gy == 15)
    def _():
        xf[37:42, 16:96] = jnp.zeros((5, 80, 128), F32)

    @pl.when(z == 0)
    def _():
        xf[:, 16:24] = jnp.zeros((42, 8, 128), F32)

    @pl.when(z == 15)
    def _():
        xf[:, 88:96] = jnp.zeros((42, 8, 128), F32)

    @pl.loop(0, 21)
    def _(t):
        rs = pl.ds(t * 2, 2)
        for p in range(4):
            lanes = slice(p * 128, p * 128 + 128)
            xs[rs, 0:32, lanes] = xf[rs, pl.ds(23 + p, 32, 2), :].astype(BF16)
            right = xf[rs, pl.ds(87 + p, 8, 2), :]
            left = xf[rs, pl.ds(7 + p, 8, 2), :]
            xs[rs, 32:48, lanes] = jnp.concatenate([right, left], axis=1).astype(BF16)

    @pl.loop(0, 5)
    def _(t):
        acc = dot(xs[pl.ds(t * 8, 8)].reshape(384, 512), w1[0])
        acc += dot(xs[pl.ds(t * 8 + 1, 8)].reshape(384, 512), w1[1])
        acc += dot(xs[pl.ds(t * 8 + 2, 8)].reshape(384, 512), w1[2])
        sig = sigmoid(acc)
        hid = (acc * sig).astype(BF16).astype(F32).reshape(4, 2, 48, 256)
        slope = sig * (1.0 + acc * (1.0 - sig))
        d1[pl.ds(t * 8, 8)] = slope.reshape(8, 48, 256)[:, 0:32]
        total = hid[:, 0] + hid[:, 1]
        total = (total[:, :, 0:128] + total[:, :, 128:256]) * 0.25
        row = lax.broadcasted_iota(jnp.int32, (4, 48, 128), 0) + (t * 4 - 2 + gy * 16)
        k = lax.broadcasted_iota(jnp.int32, (4, 48, 128), 1)
        col = jnp.where(k < 40, k, k - 48) + z * 32
        inside = (row >= 0) & (row < 256) & (col >= 0) & (col < 512)
        pooled = jnp.where(inside, total, 0.0).astype(BF16)
        pool[pl.ds(t * 4, 4)] = pooled[:, 0:32]
        mid = dot(pooled.reshape(192, 128), proj[...]).astype(BF16).astype(F32).reshape(4, 48, 256)
        mf[pl.ds(t * 4, 4), 16:56] = mid[:, 0:40]
        mf[pl.ds(t * 4, 4), 8:16] = mid[:, 40:48]

    @pl.loop(0, 10)
    def _(t):
        rs = pl.ds(t * 2, 2)
        for b in range(3):
            lanes = slice(b * 256, b * 256 + 256)
            m3[rs, 0:32, lanes] = mf[rs, 15 + b : 47 + b, :].astype(BF16)
            sides = [mf[rs, 47 + b : 55 + b, :], mf[rs, 7 + b : 15 + b, :]]
            m3[rs, 32:48, lanes] = jnp.concatenate(sides, axis=1).astype(BF16)

    @pl.loop(0, 3)
    def _(t):
        acc = dot(m3[pl.ds(t * 6, 6)].reshape(288, 768), k2[0].reshape(768, 256))
        acc += dot(m3[pl.ds(t * 6 + 1, 6)].reshape(288, 768), k2[1].reshape(768, 256))
        acc += dot(m3[pl.ds(t * 6 + 2, 6)].reshape(288, 768), k2[2].reshape(768, 256))
        sig = sigmoid(acc)
        fb[pl.ds(t * 6, 6)] = (acc * sig).astype(BF16).reshape(6, 48, 256)[:, 0:32]
        slopes[pl.ds(t * 6, 6)] = (sig * (1.0 + acc * (1.0 - sig))).reshape(6, 48, 256)


    for c in cots:
        c.wait_recv()
    cotf[1:17, 0:32] = cot_in[...].astype(F32)
    cotf[0, 0:32] = cot_rows[0].astype(F32)
    cotf[17, 0:32] = cot_rows[1].astype(F32)
    for side, at in ((0, 47), (1, 32)):
        column = cot_cols[side, 1].astype(F32)
        for q in range(16):
            cotf[1 + q, at : at + 1, :] = column[q : q + 1]
        cotf[0, at : at + 1, :] = cot_cols[side, 0].astype(F32)[15:16]
        cotf[17, at : at + 1, :] = cot_cols[side, 2].astype(F32)[0:1]

    @pl.when(gy == 0)
    def _():
        cotf[0] = jnp.zeros((48, 256), F32)

    @pl.when(gy == 15)
    def _():
        cotf[17] = jnp.zeros((48, 256), F32)

    @pl.when(z == 0)
    def _():
        cotf[:, 40:48] = jnp.zeros((18, 8, 256), F32)

    @pl.when(z == 15)
    def _():
        cotf[:, 32:40] = jnp.zeros((18, 8, 256), F32)

    @pl.loop(0, 3)
    def _(t):
        slope = (slopes[pl.ds(t * 6, 6)] * cotf[pl.ds(t * 6, 6)]).astype(BF16)
        si[pl.ds(t * 6, 6)] = slope[:, 0:32]
        slope = slope.astype(F32)
        sf[pl.ds(t * 6, 6), 16:56] = slope[:, 0:40]
        sf[pl.ds(t * 6, 6), 8:16] = slope[:, 40:48]


    for a in range(3):
        grad = dot(m3[a + 1 : a + 17, 0:32].reshape(512, 768), si[1:17].reshape(512, 256), ((0,), (0,)))
        pack[3 * a : 3 * a + 3] = grad.reshape(3, 256, 256).astype(BF16)

    mine = pl.ds(pl.multiple_of(core * 128, 128), 128)
    other = pl.ds(pl.multiple_of((1 - core) * 128, 128), 128)

    def axes(yfirst):
        if yfirst:
            return (y, lambda p: dev(x, p, core, z)), (x, lambda p: dev(p, y, core, z))
        return (x, lambda p: dev(p, y, core, z)), (y, lambda p: dev(x, p, core, z))

    def st0(ci):
        u0, n, yf = CHUNKS[ci]
        us = pl.ds(u0, n)
        return [push(pack.at[us, :, other], r0.at[us], s0s.at[ci], s0r.at[ci], sib)]

    def st1(ci, c):
        u0, n, yf = CHUNKS[ci]
        us = pl.ds(u0, n)
        c[0].wait_recv()
        h0[us] = (pack[us, :, mine].astype(F32) + r0[us].astype(F32)).astype(BF16)
        (fm, fd), _ = axes(yf)
        out_c = []
        for d in range(1, 4):
            p = mod4(fm + d)
            out_c.append(push(h0.at[us, pl.ds(pl.multiple_of(p * 64, 64), 64)], r1.at[d - 1, us], s1s.at[ci, d - 1], s1r.at[ci, d - 1], fd(p)))
        return out_c

    def st2(ci, c):
        u0, n, yf = CHUNKS[ci]
        us = pl.ds(u0, n)
        for k in c:
            k.wait_recv()
        (fm, fd), (sm, sd) = axes(yf)
        h1[us] = (h0[us, pl.ds(pl.multiple_of(fm * 64, 64), 64)].astype(F32) + r1[0, us].astype(F32) + r1[1, us].astype(F32) + r1[2, us].astype(F32)).astype(BF16)
        out_c = []
        for d in range(1, 4):
            p = mod4(sm + d)
            out_c.append(push(h1.at[us, pl.ds(pl.multiple_of(p * 16, 16), 16)], r2.at[d - 1, us], s2s.at[ci, d - 1], s2r.at[ci, d - 1], sd(p)))
        return out_c

    def st3(ci, c):
        u0, n, yf = CHUNKS[ci]
        us = pl.ds(u0, n)
        for k in c:
            k.wait_recv()
        (fm, fd), (sm, sd) = axes(yf)
        h2[us] = (h1[us, pl.ds(pl.multiple_of(sm * 16, 16), 16)].astype(F32) + r2[0, us].astype(F32) + r2[1, us].astype(F32) + r2[2, us].astype(F32)).astype(BF16)

    def rows16(yf):
        (fm, fd), (sm, sd) = axes(yf)
        return pl.ds(pl.multiple_of(fm * 64 + sm * 16, 16), 16)

    def rows64(yf):
        (fm, fd), (sm, sd) = axes(yf)
        return pl.ds(pl.multiple_of(fm * 64, 64), 64)

    def run(d):
        return dev(x, y, core, zh * 4 + mod4(zl + d))

    def za0():
        out_c = []
        for d in range(1, 4):
            p = mod4(zl + d)
            out_c.append(push(h2.at[pl.ds(p * 2, 2)], ra.at[d - 1], zas.at[0, d - 1], zar.at[0, d - 1], run(d)))
        return out_c

    def za1():
        rl[zl] = h2[8:12]
        return [push(h2.at[8:12], rl.at[zl], zas.at[1, d - 1], zar.at[1, d - 1], run(d)) for d in range(1, 4)]

    def far(src, dst, zi):
        return [push(src, dst, zbs.at[zi, d - 1], zbr.at[zi, d - 1], dev(x, y, core, lax.rem(z + 4 * d, 16))) for d in (2, 1, 3)]

    def sum4(ref):
        return ref[0].astype(F32) + ref[1].astype(F32) + ref[2].astype(F32) + ref[3].astype(F32)

    def zb0(c):
        for k in c:
            k.wait_recv()
        hz[0:2] = (h2[pl.ds(zl * 2, 2)].astype(F32) + ra[0].astype(F32) + ra[1].astype(F32) + ra[2].astype(F32)).astype(BF16)
        rb0[zh] = hz[0:2]
        pl.semaphore_wait(ready, 1)
        return far(hz.at[0:2], rb0.at[zh], 0)

    def zb1(c):
        for k in c:
            k.wait_recv()
        hz[2:6] = sum4(rl).astype(BF16)
        rb1[zh] = hz[2:6]
        return far(hz.at[2:6], rb1.at[zh], 1)

    def zc0(c):
        for k in c:
            k.wait_recv()
        flag = lax.div(zl, 2)
        r16 = pl.ds(pl.multiple_of((1 - flag) * (y * 64 + x * 16) + flag * (x * 64 + y * 16), 16), 16)
        us = pl.ds(zl * 2, 2)
        out[us, r16, mine] = sum4(rb0).astype(BF16)
        return [push(out.at[us, r16, mine], out.at[us, r16, mine], zcs.at[d - 1], zcr.at[d - 1], run(d)) for d in range(1, 4)]

    def zc1(c):
        for k in c:
            k.wait_recv()
        total = sum4(rb1).astype(BF16)
        out[8:10, rows16(True), mine] = total[0:2]
        out[10:12, rows16(False), mine] = total[2:4]

    def st5(ci):
        u0, n, yf = CHUNKS[ci]
        us = pl.ds(u0, n)
        r16 = rows16(yf)
        (fm, fd), (sm, sd) = axes(yf)
        return [push(out.at[us, r16, mine], out.at[us, r16, mine], g2s.at[ci, d - 1], g2r.at[ci, d - 1], sd(mod4(sm + d))) for d in range(1, 4)]

    def st6(ci, c):
        u0, n, yf = CHUNKS[ci]
        us = pl.ds(u0, n)
        for k in c:
            k.wait_recv()
        r64 = rows64(yf)
        (fm, fd), (sm, sd) = axes(yf)
        return [push(out.at[us, r64, mine], out.at[us, r64, mine], g1s.at[ci, d - 1], g1r.at[ci, d - 1], fd(mod4(fm + d))) for d in range(1, 4)]

    def st7(ci, c):
        u0, n, yf = CHUNKS[ci]
        us = pl.ds(u0, n)
        for k in c:
            k.wait_recv()
        return [push(out.at[us, :, mine], out.at[us, :, mine], g0s.at[ci], g0r.at[ci], sib)]


    state = [st0(0), st0(1), None, None]

    @pl.loop(0, 9)
    def _(t):
        rs = pl.ds(t * 2, 2)
        for b in range(3):
            s3[rs, :, b * 256 : b * 256 + 256] = sf[rs, 17 - b : 49 - b, :].astype(BF16)

    @pl.loop(0, 2)
    def _(t):
        acc = jnp.zeros((256, 256), F32)
        for a in range(3):
            for b in range(3):
                piece = s3[pl.ds(t * 8 + 2 - a, 8), :, b * 256 : b * 256 + 256].reshape(256, 256)
                acc += dot(piece, k2[a, b], ((1,), (1,)))
        ms[pl.ds(pl.multiple_of(t * 256, 256), 256)] = acc.astype(BF16)

    state[0] = st1(0, state[0])
    state[1] = st1(1, state[1])

    pack[11, 128:256, :] = dot(pool[2:18].reshape(512, 128), ms[...], ((0,), (0,))).astype(BF16)
    pack[11, 0:128, 128:256] = jnp.zeros((128, 128), BF16)

    @pl.loop(0, 4)
    def _(t):
        part = ms[pl.ds(pl.multiple_of(t * 128, 128), 128)]
        back = dot(part, proj[...], ((1,), (1,))).astype(BF16).astype(F32) * 0.25
        back = back.reshape(4, 32, 128)
        back = jnp.concatenate([back, back], axis=2)
        slope = d1[pl.ds(t * 8 + 4, 8)].reshape(4, 2, 32, 256)
        slope = jnp.stack([slope[:, 0] * back, slope[:, 1] * back], axis=1)
        s1[pl.ds(t * 8, 8)] = slope.reshape(8, 32, 256).astype(BF16)

    for a in range(3):
        grad = dot(xs[a + 4 : a + 36, 0:32].reshape(1024, 512), s1[...].reshape(1024, 256), ((0,), (0,)))
        for b in range(3):
            t = 3 * a + b
            tap = grad[b * 128 : b * 128 + 128, 0:128] + grad[b * 128 + 128 : b * 128 + 256, 128:256]
            pack[
                9 + t // 4, (t // 2) % 2 * 128 : (t // 2) % 2 * 128 + 128, t % 2 * 128 : t % 2 * 128 + 128
            ] = tap.astype(BF16)

    state[2], state[3] = st0(2), st0(3)
    state[0] = st2(0, state[0])
    state[1] = st2(1, state[1])
    state[2] = st1(2, state[2])
    state[3] = st1(3, state[3])
    st3(0, state[0])
    st3(1, state[1])
    first = za0()
    state[2] = st2(2, state[2])
    state[3] = st2(3, state[3])
    first = zb0(first)
    st3(2, state[2])
    st3(3, state[3])
    second = za1()
    feat_copy = push(fb.at[1:17], feat, fs, fr, near(other_sec, 0, 0))
    second = zb1(second)
    first = zc0(first)
    for c in first:
        c.wait_recv()
    state[0], state[1] = st5(0), st5(1)
    zc1(second)
    state[2], state[3] = st5(2), st5(3)
    state[0], state[1] = st6(0, state[0]), st6(1, state[1])
    state[2], state[3] = st6(2, state[2]), st6(3, state[3])
    state[0], state[1] = st7(0, state[0]), st7(1, state[1])
    state[2], state[3] = st7(2, state[2]), st7(3, state[3])
    leaves = []
    for half, (u, n) in enumerate(((0, 8), (8, 4))):
        for c in state[2 * half : 2 * half + 2]:
            for e in c:
                e.wait_recv()
        c = pltpu.make_async_copy(out.at[u : u + n], out_h.at[u : u + n], leave.at[half])
        c.start()
        leaves.append(c)
    for c in leaves:
        c.wait()
    feat_copy.wait_recv()
    for c in sends:
        c.wait_send()


def network_call(img, k1, proj, k2, cot):
    V, D = pltpu.VMEM, pltpu.SemaphoreType.DMA
    n = len(CHUNKS)
    macs = 2 * 1000 * 1000 * 1000
    return pl.pallas_call(
        network,
        out_shape=(
            jax.ShapeDtypeStruct((UNITS, 256, 256), BF16),
            jax.ShapeDtypeStruct((16, 32, 256), BF16),
        ),
        in_specs=[pl.BlockSpec(memory_space=pltpu.HBM)] * 5,
        out_specs=(pl.BlockSpec(memory_space=pltpu.HBM),) * 2,
        scratch_shapes=[
            V((UNITS, 256, 256), BF16), D((2,)),
            V((32, 64, 128), BF16), V((3, 3, 128, 128), BF16), V((128, 256), BF16),
            V((3, 3, 256, 256), BF16), V((16, 32, 256), BF16), D((5,)),
            V((42, 112, 128), F32), V((42, 48, 512), BF16), V((3, 512, 256), BF16),
            V((40, 32, 256), F32), V((20, 32, 128), BF16), V((20, 64, 256), F32),
            V((20, 48, 768), BF16), V((18, 48, 256), F32), V((18, 48, 256), F32), V((18, 64, 256), F32),
            V((18, 32, 256), BF16), V((18, 32, 768), BF16), V((512, 256), BF16),
            V((32, 32, 256), BF16), V((18, 32, 256), BF16), V((UNITS, 256, 256), BF16),
            V((2, 256, 128), BF16), V((2, 5, 64, 128), BF16), V((2, 256, 128), BF16),
            V((4, 48, 128), BF16), V((2, 16, 256), BF16), V((16, 32, 256), BF16),
            V((2, 32, 256), BF16), V((2, 3, 16, 256), BF16),
            V((UNITS, 256, 128), BF16), V((UNITS, 256, 128), BF16),
            V((3, UNITS, 64, 128), BF16), V((UNITS, 64, 128), BF16),
            V((3, UNITS, 16, 128), BF16), V((UNITS, 16, 128), BF16),
            V((3, 2, 16, 128), BF16), V((6, 16, 128), BF16), V((4, 2, 16, 128), BF16),
            V((4, 4, 16, 128), BF16), V((4, 4, 16, 128), BF16),
            D((8,)), D((8,)), D((9,)), D((9,)), D(()), D(()),
            D((n,)), D((n,)), D((n, 3)), D((n, 3)), D((n, 3)), D((n, 3)),
            D((2, 3)), D((2, 3)), D((2, 3)), D((2, 3)), D((3,)), D((3,)),
            D((n, 3)), D((n, 3)), D((n, 3)), D((n, 3)), D((n,)), D((n,)),
            pltpu.SemaphoreType.REGULAR,
        ],
        compiler_params=pltpu.CompilerParams(
            collective_id=0, has_side_effects=True, vmem_limit_bytes=56 << 20
        ),
        cost_estimate=pl.CostEstimate(
            flops=2 * macs, bytes_accessed=8 << 20, transcendentals=1 << 20
        ),
    )(img, k1, proj, k2, cot)


def widen(
    total, near, features, grad_first, grad_projection, grad_second,
    narrow, first, projection, second, feat, in_sems, out_sems,
):
    cuts = ((9, 3), (0, 3), (3, 3), (6, 3))
    loads = [
        pltpu.make_async_copy(total.at[u : u + n], narrow.at[u : u + n], in_sems.at[i])
        for i, (u, n) in enumerate(cuts)
    ] + [pltpu.make_async_copy(near, feat, in_sems.at[4])]
    for c in loads:
        c.start()
    stores = []

    def store(src, dst):
        c = pltpu.make_async_copy(src, dst, out_sems.at[len(stores)])
        c.start()
        stores.append(c)

    loads[0].wait()
    for t in range(9):
        row, lane = (t // 2) % 2 * 128, t % 2 * 128
        first[t // 3, t % 3] = narrow[9 + t // 4, row : row + 128, lane : lane + 128].astype(F32)
    projection[...] = narrow[11, 128:256, :].astype(F32)
    store(first, grad_first)
    store(projection, grad_projection)
    for a in range(3):
        loads[1 + a].wait()
        for b in range(3):
            second[a, b] = narrow[3 * a + b].astype(F32)
        store(second.at[a], grad_second.at[a])
    loads[4].wait()
    store(feat, features.at[0])
    for c in stores:
        c.wait()


def per_device(images, first_kernel, projection, second_kernel, cotangent):
    total, features = network_call(images[0], first_kernel, projection, second_kernel, cotangent[0])
    features, grad_first, grad_projection, grad_second = pl.pallas_call(
        widen,
        out_shape=(
            jax.ShapeDtypeStruct((1, 16, 32, 256), BF16),
            jax.ShapeDtypeStruct((3, 3, 128, 128), F32),
            jax.ShapeDtypeStruct((128, 256), F32),
            jax.ShapeDtypeStruct((3, 3, 256, 256), F32),
        ),
        in_specs=[pl.BlockSpec(memory_space=pltpu.HBM)] * 2,
        out_specs=(pl.BlockSpec(memory_space=pltpu.HBM),) * 4,
        scratch_shapes=[
            pltpu.VMEM((UNITS, 256, 256), BF16), pltpu.VMEM((3, 3, 128, 128), F32),
            pltpu.VMEM((128, 256), F32), pltpu.VMEM((3, 3, 256, 256), F32),
            pltpu.VMEM((16, 32, 256), BF16),
            pltpu.SemaphoreType.DMA((5,)), pltpu.SemaphoreType.DMA((6,)),
        ],
        compiler_params=pltpu.CompilerParams(vmem_limit_bytes=60 << 20),
    )(total, features)
    return (features, grad_first, grad_projection, grad_second)


def solution(mesh):
    placed = (P("section", "gy", "gx", None), P(), P(), P(), P("section", "gy", "gx", None))
    return jax.shard_map(
        per_device,
        mesh=mesh,
        in_specs=placed,
        out_specs=(P("section", "gy", "gx", None), P(), P(), P()),
        check_vma=False,
    )
```
